128 devices in a mesh: seq: 8 (over x, core), head: 16 (over y, z).
Axes of the slice: x: 4, y: 4, z: 4, core: 2. Of those that a mesh axis runs over, the one named last changes fastest.
Arguments:
- qk_in: bfloat16 [4, 8192, 2, 2048], P(None, 'seq', None, 'head'), may hold values from -6 to 6
- v_in: bfloat16 [4, 8192, 4096], P(None, 'seq', 'head'), may hold values from -6 to 6
- gate_z: bfloat16 [4, 8192, 4096], P(None, 'seq', 'head'), may hold values from -6 to 6
- conv_qk: bfloat16 [4, 2, 2048], P(None, None, 'head'), may hold values from -3 to 3
- conv_v: bfloat16 [4, 4096], P(None, 'head'), may hold values from -3 to 3
- log_decay: float32 [4, 32, 8192], P(None, 'head', 'seq'), may hold values from -0.7 to 0
- write_gain: float32 [4, 32, 8192], P(None, 'head', 'seq'), may hold values from 0 to 1
- norm_gain: float32 [128], replicated, may hold values from 0.5 to 1.5
- prompt_lengths: int32 [4], replicated, may hold values from 1 to 8192, 20480 in all
- placement: int32 [8, 16], P('seq'), may hold values from 0 to 3
Outputs:
- attended: bfloat16 [4, 8192, 4096], P(None, 'seq', 'head')
- rollout_state: float32 [8, 16, 32, 128, 128], P('seq', 'head')
The draws below stay inside these ranges and needn't reach their ends.
Inputs may be any that keep to these rules, and one draw needn't show every extreme that they name: `prompt_lengths`: the largest length is exactly 8192; the lengths sum to 20480. Device (s, r) serves prompt placement[s, r]; the values 0 and 3 each occur at least once.
All inputs are finite; a program needn't handle non-finite values.
Results may differ from the reference program's by a relative error of at most 0.02.
Values may be sent and summed in bfloat16 or wider, within the bound.
A program may use at most 128 MiB of HBM per device.

```python
import math
import jax
import jax.numpy as jnp
import numpy as np
from jax import lax

VALUE_HEAD_COUNT = 32
HK = 16
DK = 128
DV = 128
CONV = 4
SPAN = 64
PROMPT_COUNT = 4
TOK_DEV = 1024
PROMPT_LENGTH = 8192
N_SEQ = 8
N_HEAD = 16


def head_speed(key, fast_share):
    marks = jax.random.uniform(jax.random.fold_in(key, 77), (PROMPT_COUNT, VALUE_HEAD_COUNT, 1), jnp.float32)
    return (marks < fast_share).astype(jnp.float32)


def draw_log_decay(key, part):
    fast_mask = head_speed(key, 0.5)
    key = jax.random.fold_in(key, 1)
    random_subkeys = jax.random.split(key, 6)
    quick_rate = jax.random.uniform(random_subkeys[0], (PROMPT_COUNT, VALUE_HEAD_COUNT, 1), jnp.float32, 1.0 / 50.0, 1.0 / 30.0)
    slow_rate = 0.15 / PROMPT_LENGTH * jnp.exp(jax.random.uniform(random_subkeys[1], (PROMPT_COUNT, VALUE_HEAD_COUNT, 1), jnp.float32, -0.7, 0.7))
    base_rate = jnp.where(fast_mask > 0.5, quick_rate, slow_rate)
    roughness = jax.random.uniform(random_subkeys[2], (PROMPT_COUNT, VALUE_HEAD_COUNT, PROMPT_LENGTH), jnp.float32, 0.4, 1.6)
    segments = jnp.exp(jax.random.uniform(random_subkeys[3], (PROMPT_COUNT, VALUE_HEAD_COUNT, PROMPT_LENGTH // TOK_DEV, 1), jnp.float32, -0.7, 0.7))
    segments = jnp.broadcast_to(segments, (PROMPT_COUNT, VALUE_HEAD_COUNT, PROMPT_LENGTH // TOK_DEV, TOK_DEV)).reshape(PROMPT_COUNT, VALUE_HEAD_COUNT, PROMPT_LENGTH)
    smoothing_factor = -base_rate * roughness * segments
    spike_mask = jax.random.uniform(random_subkeys[4], (PROMPT_COUNT, VALUE_HEAD_COUNT, PROMPT_LENGTH), jnp.float32) < 2.0 / PROMPT_LENGTH
    spike_removal = jax.random.uniform(random_subkeys[5], (PROMPT_COUNT, VALUE_HEAD_COUNT, PROMPT_LENGTH), jnp.float32, -0.69, -0.23)
    return jnp.where(spike_mask, spike_removal, smoothing_factor)


def draw_write_gain(key, part):
    fast_mask = head_speed(key, 0.5)
    key = jax.random.fold_in(key, 2)
    random_subkeys = jax.random.split(key, 2)
    quick_beta = jax.random.uniform(random_subkeys[0], (PROMPT_COUNT, VALUE_HEAD_COUNT, PROMPT_LENGTH), jnp.float32, 0.2, 0.95)
    slow_scale = min(0.5, 32.0 / PROMPT_LENGTH)
    slow_beta = slow_scale * jax.random.uniform(random_subkeys[1], (PROMPT_COUNT, VALUE_HEAD_COUNT, PROMPT_LENGTH), jnp.float32, 0.4, 1.6)
    return jnp.where(fast_mask > 0.5, quick_beta, slow_beta)


def with_ends(values, rng, smallest, high):
    shape = values.shape
    place = [jax.random.randint(jax.random.fold_in(rng, axis), (), 0, shape[axis]) for axis in range(len(shape))]
    values = values.at[tuple(place)].set(smallest)
    longest = shape.index(max(shape))
    place[longest] = (place[longest] + 1) % shape[longest]
    return values.at[tuple(place)].set(high)


def block_levels(stream_key, extent, pieces, smallest, top_value):
    loudness = 1.0
    for axis_at, shards_of in pieces:
        heights = jax.random.uniform(jax.random.fold_in(jax.random.fold_in(stream_key, 6), axis_at), (shards_of,), jnp.float32, smallest / len(pieces), top_value / len(pieces))
        loudness = loudness * jnp.repeat(jnp.exp(heights), extent[axis_at] // shards_of).reshape((-1,) + (1,) * (len(extent) - 1 - axis_at))
    return loudness


def rank_bounds(amount, skew):
    loads = [(1 << 20) // math.isqrt(rank ** skew) + 1 for rank in range(1, amount + 1)]
    scale = 1 + sum(loads) // (1 << 30)
    return np.cumsum(np.array([max(1, weight // scale) for weight in loads]))


def ranked_ids(rng, shape, amount, skew):
    grid = rank_bounds(amount, skew)
    lot = jax.random.randint(jax.random.fold_in(rng, 1), shape, 0, int(grid[amount - 1]))
    standing = jnp.searchsorted(jnp.asarray(grid, jnp.int32), lot, side="right")
    return jax.random.permutation(jax.random.fold_in(rng, 2), amount)[standing].astype(jnp.int32)


def profile(count, total, bound, slope):
    weights = [(1 << 20) // math.isqrt(rank ** slope) + 1 for rank in range(2, count + 1)]
    rest, given = total - bound - (count - 1), [1] * (count - 1)
    while rest > 0:
        free = [i for i in range(count - 1) if given[i] < bound]
        whole, left = sum([weights[i] for i in free]), rest
        for i in free:
            extra = min(bound - given[i], max(1, left * weights[i] // whole), rest)
            given[i] = given[i] + extra
            rest = rest - extra
    return np.array([bound] + given)


def ragged(stream_key, count, total, most, slope):
    if count == 2:
        one = jax.random.randint(stream_key, (), max(1, total - most), min(most, total - 1) + 1)
        return jnp.stack([one, total - one])
    tallies = jnp.asarray(profile(count, total, most, slope), jnp.int32)
    twos = (count - 1) // 2
    donor, sink = tallies[1:1 + 2 * twos:2], tallies[2:2 + 2 * twos:2]
    slack = jnp.minimum(donor - 1, most - sink)
    shifted = jax.random.randint(jax.random.fold_in(stream_key, 1), (twos,), 0, 1 << 20) % (slack + 1)
    tallies = tallies.at[1:1 + 2 * twos:2].set(donor - shifted).at[2:2 + 2 * twos:2].set(sink + shifted)
    return tallies[jax.random.permutation(jax.random.fold_in(stream_key, 2), count)]


def bell_draw(stream_key, shape, scale, limit, cuts=(), kind=jnp.bfloat16):
    values = jax.random.normal(stream_key, shape, jnp.float32) * scale
    if len(cuts) > 0:
        values = block_levels(stream_key, shape, cuts, -0.22, 0.18) * values
    return jnp.clip(values, min=-limit, max=limit).astype(kind)


def setup_inputs(seed: int = 0) -> dict:
    key_list = jax.random.split(jax.random.key(seed), 11)
    return {
        "qk_in": bell_draw(key_list[0], (PROMPT_COUNT, PROMPT_LENGTH, 2, HK * DK), 1.0, 6.0, ((1, 8), (3, 16))),
        "v_in": bell_draw(key_list[1], (PROMPT_COUNT, PROMPT_LENGTH, VALUE_HEAD_COUNT * DV), 1.0, 6.0, ((1, 8), (2, 16))),
        "gate_z": bell_draw(key_list[2], (PROMPT_COUNT, PROMPT_LENGTH, VALUE_HEAD_COUNT * DV), 1.0, 6.0, ((1, 8), (2, 16))),
        "conv_qk": bell_draw(key_list[3], (CONV, 2, HK * DK), CONV ** -0.5, 3.0, ((2, 16),)),
        "conv_v": bell_draw(key_list[4], (CONV, VALUE_HEAD_COUNT * DV), CONV ** -0.5, 3.0, ((1, 16),)),
        "log_decay": draw_log_decay(jax.random.fold_in(key_list[10], 71), 0),
        "write_gain": draw_write_gain(jax.random.fold_in(key_list[10], 71), 0),
        "norm_gain": jnp.clip(1.0 + 0.1 * jax.random.normal(key_list[7], (DV,), jnp.float32), 0.5, 1.5),
        "prompt_lengths": ragged(key_list[8], PROMPT_COUNT, PROMPT_COUNT * PROMPT_LENGTH * 5 // 8, PROMPT_LENGTH, 1).astype(jnp.int32),
        "placement": with_ends(ranked_ids(key_list[9], (N_SEQ, N_HEAD), PROMPT_COUNT, 2), jax.random.fold_in(key_list[9], 3), 0, PROMPT_COUNT - 1).astype(jnp.int32),
    }


TOP_PRECISION = lax.Precision.HIGHEST
EPSILON = 1e-06

def unit_lower_inverse(strict):
    length = strict.shape[-1]
    identity_matrix = jnp.eye(length, dtype=jnp.float32)
    power_term = -strict
    result = identity_matrix + power_term
    for section_index in range(1, length.bit_length() - 1):
        power_term = jnp.matmul(power_term, power_term, precision=TOP_PRECISION)
        result = result + jnp.matmul(result, power_term, precision=TOP_PRECISION)
    return result

def causal_conv(previous, current, conv_weight):
    joined = jnp.concatenate([previous, current], axis=1).astype(jnp.float32)
    length = current.shape[1]
    taps_count = conv_weight.shape[0]
    tap_weights = conv_weight.astype(jnp.float32)
    summed = joined[:, 0:length] * tap_weights[0]
    for offset in range(1, taps_count):
        summed = summed + joined[:, offset:offset + length] * tap_weights[offset]
    return jax.nn.silu(summed)

def unit_rows(row_block):
    return row_block / jnp.sqrt(lax.optimization_barrier(jnp.sum(row_block * row_block, axis=-1, keepdims=True)) + EPSILON)

def wide(tensor):
    return tensor.astype(jnp.float32)

def reference(qk_in, v_in, gate_z, conv_qk, conv_v, log_decay, write_gain, norm_gain, prompt_lengths, placement):
    group_size = VALUE_HEAD_COUNT // HK
    blocks = PROMPT_LENGTH // SPAN
    positions = jnp.arange(PROMPT_LENGTH, dtype=jnp.int32)
    lower_incl = jnp.tril(jnp.ones((SPAN, SPAN), dtype=bool))
    lower_strict = jnp.tril(jnp.ones((SPAN, SPAN), dtype=bool), -1)

    def advance(present_state, inputs):
        block_queries, key_block, value_block, gate_block, gain_block = inputs
        running_total = jnp.cumsum(gate_block, axis=-1)
        spread = running_total[:, :, None] - running_total[:, None, :]
        decay_ratio = jnp.where(lower_incl, jnp.exp(jnp.where(lower_incl, spread, 0.0)), 0.0)
        key_key = jnp.einsum('hik,hjk->hij', wide(key_block), wide(key_block), precision=TOP_PRECISION)
        query_key = jnp.einsum('hik,hjk->hij', wide(block_queries), wide(key_block), precision=TOP_PRECISION)
        strict = jnp.where(lower_strict, gain_block[:, :, None] * decay_ratio * key_key, 0.0)
        inverse = unit_lower_inverse(strict).astype(jnp.bfloat16)
        faded_state = jnp.exp(running_total)
        scaled_keys = (wide(key_block) * (gain_block * faded_state)[:, :, None]).astype(jnp.bfloat16)
        scaled_values = (wide(value_block) * gain_block[:, :, None]).astype(jnp.bfloat16)
        w_rows = jnp.einsum('hij,hjk->hik', wide(inverse), wide(scaled_keys), precision=TOP_PRECISION).astype(jnp.bfloat16)
        u_rows = jnp.einsum('hij,hjv->hiv', wide(inverse), wide(scaled_values), precision=TOP_PRECISION).astype(jnp.bfloat16)
        start = present_state.astype(jnp.bfloat16)
        fresh = (wide(u_rows) - jnp.einsum('xtc,xcy->xty', wide(w_rows), wide(start), precision=TOP_PRECISION)).astype(jnp.bfloat16)
        scores = (decay_ratio * query_key).astype(jnp.bfloat16)
        state_contribution = jnp.einsum('xtc,xcy->xty', wide(block_queries), wide(start), precision=TOP_PRECISION) * faded_state[:, :, None]
        outputs = state_contribution + jnp.einsum('hij,hjv->hiv', wide(scores), wide(fresh), precision=TOP_PRECISION)
        trailing_keys = (wide(key_block) * jnp.exp(running_total[:, -1:] - running_total)[:, :, None]).astype(jnp.bfloat16)
        following_state = jnp.exp(running_total[:, -1])[:, None, None] * present_state + jnp.einsum('sjb,sjf->sbf', wide(trailing_keys), wide(fresh), precision=TOP_PRECISION)
        return (following_state, outputs)

    def blocked(tensor):
        return jnp.transpose(tensor.reshape(blocks, SPAN, VALUE_HEAD_COUNT, tensor.shape[-1]), (0, 2, 1, 3))

    def blocked_gate(tensor):
        return jnp.transpose(tensor.reshape(VALUE_HEAD_COUNT, blocks, SPAN), (1, 0, 2))

    def one_prompt(inputs):
        qk_raw, v_raw, z_raw, log_row, gain_row, length = inputs
        is_valid = positions < length
        zeros_qk = jnp.zeros((1, CONV - 1, 2, HK * DK), jnp.bfloat16)
        zeros_v = jnp.zeros((1, CONV - 1, VALUE_HEAD_COUNT * DV), jnp.bfloat16)
        qk_mixed = causal_conv(zeros_qk, qk_raw[None], conv_qk)[0]
        v_mixed = causal_conv(zeros_v, v_raw[None], conv_v)[0].astype(jnp.bfloat16)
        queries = jnp.repeat(unit_rows(qk_mixed[:, 0].reshape(PROMPT_LENGTH, HK, DK)).astype(jnp.bfloat16), group_size, axis=1)
        keys_all = jnp.repeat(unit_rows(qk_mixed[:, 1].reshape(PROMPT_LENGTH, HK, DK)).astype(jnp.bfloat16), group_size, axis=1)
        values = v_mixed.reshape(PROMPT_LENGTH, VALUE_HEAD_COUNT, DV)
        log_gate = jnp.where(is_valid[None, :], log_row, 0.0)
        gain_rows = jnp.where(is_valid[None, :], gain_row, 0.0)
        zero_state = jnp.zeros((VALUE_HEAD_COUNT, DK, DV), jnp.float32)
        final_state, outputs = lax.scan(advance, zero_state, (blocked(queries), blocked(keys_all), blocked(values), blocked_gate(log_gate), blocked_gate(gain_rows)))
        raw_out = jnp.transpose(outputs, (0, 2, 1, 3)).reshape(PROMPT_LENGTH, VALUE_HEAD_COUNT, DV)
        scaled = raw_out * lax.rsqrt(lax.optimization_barrier(jnp.mean(raw_out * raw_out, axis=-1, keepdims=True)) + EPSILON)
        gated = scaled * norm_gain * jax.nn.silu(z_raw.astype(jnp.float32).reshape(PROMPT_LENGTH, VALUE_HEAD_COUNT, DV))
        attended = jnp.where(is_valid[:, None, None], gated, 0.0).reshape(PROMPT_LENGTH, VALUE_HEAD_COUNT * DV).astype(jnp.bfloat16)
        return (attended, final_state)
    attended, finals = lax.map(one_prompt, (qk_in, v_in, gate_z, log_decay, write_gain, prompt_lengths))
    rollout = jnp.take(finals, placement, axis=0)
    return (attended, rollout)
```

```python
import functools

import jax
import jax.numpy as jnp
from jax import lax
from jax.experimental import pallas as pl
from jax.experimental.pallas import tpu as pltpu
from jax.sharding import PartitionSpec as P

DK = 128
DV = 128
CONV = 4
BLOCK = 128
BASE = 16
UNROLL = 4
RIM = 8
EPSILON = 1e-06
F32 = jnp.float32
BF16 = jnp.bfloat16
VMEM_LIMIT = 56 * 1024 * 1024


def dot(a, b):
    return jnp.dot(a, b, preferred_element_type=F32)


def silu(x):
    half = 0.5 * x
    return half + half * jnp.tanh(half)


def unit_inverses(stricts):
    lane = lax.broadcasted_iota(jnp.int32, (BASE, BLOCK), 1)
    row = lax.broadcasted_iota(jnp.int32, (BASE, BLOCK), 0)
    home = lane // BASE
    count = BLOCK // BASE
    lows = [s.astype(BF16) for s in stricts]
    compact = []
    for s in stricts:
        c = s[0:BASE]
        for b in range(1, count):
            c = jnp.where(home == b, s[b * BASE : (b + 1) * BASE], c)
        compact.append(c)
    eye = jnp.where(lane % BASE == row, 1.0, 0.0).astype(F32)
    xs = [eye for _ in stricts]
    for j in range(BASE - 1):
        index = home * BASE + j
        for n, c in enumerate(compact):
            column = jnp.take_along_axis(c, index, axis=1)
            xs[n] = xs[n] - column * xs[n][j : j + 1]
    slabs = []
    for x in xs:
        slabs.append([jnp.where(home == b, x, 0.0).astype(BF16) for b in range(count)])
    size = BASE
    while size < BLOCK:
        per = size // BASE
        lane_slab = lax.broadcasted_iota(jnp.int32, (size, BLOCK), 1) // size
        odd = [o for o in range(1, BLOCK // size, 2)]
        lefts = [
            jnp.concatenate([slab for o in odd for slab in sl[o * per : (o + 1) * per]], axis=0)
            for sl in slabs
        ]
        wholes = [jnp.concatenate(sl, axis=0) for sl in slabs]
        keep = jnp.concatenate([(lane_slab == o - 1).astype(F32) for o in odd], axis=0) > 0.5
        ys = [jnp.where(keep, dot(a, low), 0.0).astype(BF16) for a, low in zip(lefts, lows)]
        zs = [dot(y, w) for y, w in zip(ys, wholes)]
        for n, z in enumerate(zs):
            new = (lefts[n].astype(F32) - z).astype(BF16)
            for m, o in enumerate(odd):
                for i in range(per):
                    at = m * size + i * BASE
                    slabs[n][o * per + i] = new[at : at + BASE]
        size *= 2
    return [jnp.concatenate(sl, axis=0) for sl in slabs]


def maps_kernel(
    first_ref,
    len_ref,
    qk_ref,
    v_ref,
    rim_ref,
    cqk_ref,
    cv_ref,
    ld_ref,
    wg_ref,
    m_ref,
    out_ref,
    st_ref,
    xqk,
    xv,
    rows,
    gates,
    aq,
    binp,
    base_out,
    carry,
):
    p = pl.program_id(0)
    prompts = pl.num_programs(0)
    tok = v_ref.shape[1]
    nblk = tok // BLOCK
    heads = ld_ref.shape[1]

    xqk[0:RIM, :] = rim_ref[0, 0:RIM, :].astype(F32)
    xqk[RIM:, :] = qk_ref[0].astype(F32)
    for h in range(heads):
        lanes = slice(h * DV, (h + 1) * DV)
        xv[h, 0:RIM, :] = rim_ref[0, (1 + h) * RIM : (2 + h) * RIM, :].astype(F32)
        xv[h, RIM:, :] = v_ref[0, :, lanes].astype(F32)

    position = lax.broadcasted_iota(jnp.int32, (heads, tok), 1) + first_ref[0]
    valid = position < len_ref[p]
    log_gate = jnp.where(valid, ld_ref[0], 0.0)
    gain = jnp.where(valid, wg_ref[0], 0.0)
    rows[...] = jnp.zeros_like(rows)
    for c in range(nblk):
        rows[8 * c : 8 * c + heads, :] = log_gate[:, c * BLOCK : (c + 1) * BLOCK]
        rows[8 * c + heads : 8 * c + 2 * heads, :] = gain[:, c * BLOCK : (c + 1) * BLOCK]
    before = lax.broadcasted_iota(jnp.int32, (BLOCK, BLOCK), 0)
    after = lax.broadcasted_iota(jnp.int32, (BLOCK, BLOCK), 1)
    upto = jnp.where(before <= after, 1.0, 0.0).astype(F32)
    raw_rows = rows[...]
    sums = jnp.dot(raw_rows, upto, precision=lax.Precision.HIGHEST, preferred_element_type=F32)
    kind = lax.broadcasted_iota(jnp.int32, raw_rows.shape, 0) % 8
    rows[...] = jnp.where(kind < heads, sums, raw_rows)

    lower = before >= after
    strictly = before > after
    taps_qk = cqk_ref[...].astype(F32)
    taps_v = cv_ref[...].astype(F32)

    def group(g, _):
        blocks = range(UNROLL)
        queries, keys, keys_t, values, tiles, columns = [], [], [], [], [], []
        for u in blocks:
            c = g * UNROLL + u
            start = c * BLOCK

            def mixed(which):
                total = None
                for i in range(CONV):
                    at = RIM + 2 * (start - (CONV - 1) + i) + which
                    term = xqk[pl.ds(at, BLOCK, stride=2), :] * taps_qk[i, which : which + 1, :]
                    total = term if total is None else total + term
                return silu(total)

            def unit(x):
                return x * lax.rsqrt(jnp.sum(x * x, axis=-1, keepdims=True) + EPSILON)

            q = unit(mixed(0))
            k = unit(mixed(1))
            queries.append(q.astype(BF16))
            keys.append(k.astype(BF16))
            keys_t.append(k.T.astype(BF16))
            vs = []
            for h in range(heads):
                total = None
                for i in range(CONV):
                    at = RIM + start - (CONV - 1) + i
                    term = xv[h, pl.ds(at, BLOCK), :] * taps_v[i : i + 1, h * DV : (h + 1) * DV]
                    total = term if total is None else total + term
                vs.append(silu(total).astype(BF16))
            values.append(vs)
            tile = rows[pl.ds(pl.multiple_of(8 * c, 8), 8), :]
            tiles.append(tile)
            columns.append(tile.T)
        grams = [
            dot(jnp.concatenate([queries[u], keys[u]], axis=0), keys_t[u]) for u in blocks
        ]
        stricts, scores, fades, gains = [], [], [], []
        for u in blocks:
            query_key = grams[u][:BLOCK]
            key_key = jnp.where(strictly, grams[u][BLOCK:], 0.0)
            for h in range(heads):
                cum = jnp.broadcast_to(columns[u][:, h : h + 1], (BLOCK, BLOCK))
                gb = jnp.broadcast_to(columns[u][:, heads + h : heads + h + 1], (BLOCK, BLOCK))
                ratio = jnp.exp(jnp.where(lower, cum - tiles[u][h : h + 1], -1e30))
                stricts.append(ratio * key_key * gb)
                scores.append((ratio * query_key).astype(BF16))
                fades.append(jnp.exp(cum))
                gains.append(gb)
        inverses = unit_inverses(stricts)
        writes = []
        for u in blocks:
            for h in range(heads):
                n = u * heads + h
                scaled_k = (keys[u].astype(F32) * (gains[n] * fades[n])).astype(BF16)
                scaled_v = (values[u][h].astype(F32) * gains[n]).astype(BF16)
                both = jnp.concatenate([scaled_k, scaled_v], axis=1)
                writes.append(dot(inverses[n], both).astype(BF16))
        for u in blocks:
            for h in range(heads):
                n = u * heads + h
                cum_row = tiles[u][h : h + 1]
                last = cum_row[:, BLOCK - 1 : BLOCK]
                tails = (keys_t[u].astype(F32) * jnp.exp(last - cum_row)).astype(BF16)
                r = dot(jnp.concatenate([tails, scores[n]], axis=0), writes[n])
                at = (p * heads + h) * nblk + g * UNROLL + u
                aq[at, 0:DK, :] = (-r[:DK, :DK]).astype(BF16)
                binp[at] = r[:DK, DK:]
                aq[at, DK:, :] = (queries[u].astype(F32) * fades[n] - r[DK:, :DK]).astype(BF16)
                base_out[at] = r[DK:, DK:]
                gates[pl.ds(at, 1), :] = jnp.broadcast_to(jnp.exp(last), (1, BLOCK))
        return 0

    lax.fori_loop(0, nblk // UNROLL, group, 0)

    @pl.when(p == prompts - 1)
    def _():
        chains = carry.shape[0]
        for n in range(chains):
            at = n * nblk
            gate = gates[at : at + 1, :]
            carry[n, :, DK:] = binp[at]
            carry[n, :, :DK] = jnp.where(before == after, gate, 0.0) + aq[at, 0:DK, :].astype(F32)
            m_ref[n, 0:BLOCK, :] = aq[at, DK:, :]
            out_ref[n, 0:BLOCK, :] = base_out[at].astype(BF16)

        def step(c, _):
            for n in range(chains):
                at = n * nblk + c
                state = carry[n]
                r = dot(aq[at], state.astype(BF16))
                gate = gates[pl.ds(at, 1), :]
                carry[n, :, :DK] = gate * state[:, :DK] + r[:DK, :DK]
                carry[n, :, DK:] = gate * state[:, DK:] + r[:DK, DK:] + binp[at]
                tokens = pl.ds(pl.multiple_of(c * BLOCK, BLOCK), BLOCK)
                m_ref[n, tokens, :] = r[DK:, :DK].astype(BF16)
                out_ref[n, tokens, :] = (r[DK:, DK:] + base_out[at]).astype(BF16)
            return 0

        lax.fori_loop(1, nblk, step, 0)
        for n in range(chains):
            st_ref[n] = carry[n].astype(BF16)


def local_maps(first, lengths, qk, v, rim, conv_qk, conv_v, log_decay, write_gain):
    prompts, tok = v.shape[:2]
    heads = log_decay.shape[1]
    chains = prompts * heads
    nblk = tok // BLOCK
    units = chains * nblk

    def per_prompt(*shape):
        return pl.BlockSpec((1,) + shape, lambda p: (p,) + (0,) * len(shape))

    def whole(*shape):
        return pl.BlockSpec(shape, lambda p: (0,) * len(shape))

    smem = pl.BlockSpec(memory_space=pltpu.SMEM)
    return pl.pallas_call(
        maps_kernel,
        grid=(prompts,),
        in_specs=[
            smem,
            smem,
            per_prompt(2 * tok, DK),
            per_prompt(tok, heads * DV),
            per_prompt((1 + heads) * RIM, DK),
            whole(*conv_qk.shape),
            whole(*conv_v.shape),
            per_prompt(heads, tok),
            per_prompt(heads, tok),
        ],
        out_specs=[
            whole(chains, tok, DK),
            whole(chains, tok, DV),
            whole(chains, DK, DK + DV),
        ],
        out_shape=[
            jax.ShapeDtypeStruct((chains, tok, DK), BF16),
            jax.ShapeDtypeStruct((chains, tok, DV), BF16),
            jax.ShapeDtypeStruct((chains, DK, DK + DV), BF16),
        ],
        scratch_shapes=[
            pltpu.VMEM((RIM + 2 * tok, DK), F32),
            pltpu.VMEM((heads, RIM + tok, DV), F32),
            pltpu.VMEM((8 * nblk, BLOCK), F32),
            pltpu.VMEM((units, BLOCK), F32),
            pltpu.VMEM((units, 2 * BLOCK, DK), BF16),
            pltpu.VMEM((units, DK, DV), F32),
            pltpu.VMEM((units, BLOCK, DV), F32),
            pltpu.VMEM((chains, DK, DK + DV), F32),
        ],
        compiler_params=pltpu.CompilerParams(vmem_limit_bytes=VMEM_LIMIT),
        name="local_maps",
    )(first, lengths, qk, v, rim, conv_qk, conv_v, log_decay, write_gain)


def finish_kernel(first_ref, len_ref, maps_ref, m_ref, local_ref, z_ref, norm_ref, att_ref, final_ref):
    p = pl.program_id(0)
    count, heads = maps_ref.shape[:2]
    tok = z_ref.shape[1]
    mine = first_ref[0] // tok
    norm_gain = norm_ref[...]
    states = [jnp.zeros((DK, DV), F32) for _ in range(heads)]
    enters = [jnp.zeros((DK, DV), F32) for _ in range(heads)]
    for k in range(count):
        for h in range(heads):
            enters[h] = jnp.where(mine == k, states[h], enters[h])
            st = maps_ref[k, h]
            states[h] = dot(st[:, :DK], states[h].astype(BF16)) + st[:, DK:].astype(F32)
    for h in range(heads):
        final_ref[h] = states[h].astype(BF16)
    enters = [e.astype(BF16) for e in enters]
    step = 128

    def tokens(i, _):
        at = pl.ds(pl.multiple_of(i * step, step), step)
        position = first_ref[0] + i * step + lax.broadcasted_iota(jnp.int32, (step, DV), 0)
        valid = position < len_ref[p]
        for h in range(heads):
            raw = dot(m_ref[h, at, :], enters[h]) + local_ref[h, at, :].astype(F32)
            scaled = raw * lax.rsqrt(jnp.mean(raw * raw, axis=-1, keepdims=True) + EPSILON)
            z = z_ref[0, at, h * DV : (h + 1) * DV].astype(F32)
            gated = scaled * norm_gain * silu(z)
            att_ref[0, at, h * DV : (h + 1) * DV] = jnp.where(valid, gated, 0.0).astype(BF16)
        return 0

    lax.fori_loop(0, tok // step, tokens, 0, unroll=2)


def finish(first, lengths, maps, m, local, gate_z, norm_gain):
    prompts, tok, width = gate_z.shape
    heads = width // DV
    count = maps.shape[0]
    smem = pl.BlockSpec(memory_space=pltpu.SMEM)
    return pl.pallas_call(
        finish_kernel,
        grid=(prompts,),
        in_specs=[
            smem,
            smem,
            pl.BlockSpec((count, heads, DK, DK + DV), lambda p: (0, p, 0, 0)),
            pl.BlockSpec((heads, tok, DK), lambda p: (p, 0, 0)),
            pl.BlockSpec((heads, tok, DV), lambda p: (p, 0, 0)),
            pl.BlockSpec((1, tok, width), lambda p: (p, 0, 0)),
            pl.BlockSpec((1, DV), lambda p: (0, 0)),
        ],
        out_specs=[
            pl.BlockSpec((1, tok, width), lambda p: (p, 0, 0)),
            pl.BlockSpec((heads, DK, DV), lambda p: (p, 0, 0)),
        ],
        out_shape=[
            jax.ShapeDtypeStruct((prompts, tok, width), BF16),
            jax.ShapeDtypeStruct((prompts * heads, DK, DV), BF16),
        ],
        compiler_params=pltpu.CompilerParams(vmem_limit_bytes=VMEM_LIMIT),
        name="finish",
    )(first, lengths, maps, m, local, gate_z, norm_gain)


def shards(
    qk_in,
    v_in,
    gate_z,
    conv_qk,
    conv_v,
    log_decay,
    write_gain,
    norm_gain,
    prompt_lengths,
    placement,
):
    prompts, tok = v_in.shape[:2]
    heads = log_decay.shape[1]
    head_count = lax.axis_size("head")
    seq_count = lax.axis_size("seq")
    qk = qk_in.reshape(prompts, 2 * tok, DK)
    tails = jnp.concatenate(
        [qk[:, 2 * tok - RIM :]]
        + [v_in[:, tok - RIM :, h * DV : (h + 1) * DV] for h in range(heads)],
        axis=1,
    )
    rim = lax.ppermute(tails, "seq", [(i, i + 1) for i in range(seq_count - 1)])
    first = (lax.axis_index("seq") * tok).astype(jnp.int32).reshape(1)
    m, local, st = local_maps(
        first, prompt_lengths, qk, v_in, rim, conv_qk, conv_v, log_decay, write_gain
    )
    maps = lax.all_gather(st, "seq")
    attended, finals = finish(
        first, prompt_lengths, maps, m, local, gate_z, norm_gain.reshape(1, DV)
    )
    by_prompt = finals.reshape(prompts, heads, DK, DV)
    leaving = jnp.take(by_prompt, placement[0], axis=0)
    arrived = lax.all_to_all(leaving, "head", 0, 0, tiled=True)
    rollout = arrived.astype(F32).reshape(1, 1, head_count * heads, DK, DV)
    return attended, rollout


def solution(mesh):
    return jax.shard_map(
        shards,
        mesh=mesh,
        in_specs=(
            P(None, "seq", None, "head"),
            P(None, "seq", "head"),
            P(None, "seq", "head"),
            P(None, None, "head"),
            P(None, "head"),
            P(None, "head", "seq"),
            P(None, "head", "seq"),
            P(),
            P(),
            P("seq", None),
        ),
        out_specs=(P(None, "seq", "head"), P("seq", "head", None, None, None)),
        check_vma=False,
    )
```

```python
import functools

import jax
import jax.numpy as jnp
from jax import lax
from jax.experimental import pallas as pl
from jax.experimental.pallas import tpu as pltpu
from jax.sharding import PartitionSpec as P

DK = 128
DV = 128
CONV = 4
BLOCK = 128
BASE = 16
UNROLL = 4
RIM = 8
EPSILON = 1e-06
F32 = jnp.float32
BF16 = jnp.bfloat16
VMEM_LIMIT = 56 * 1024 * 1024


def dot(a, b):
    return jnp.dot(a, b, preferred_element_type=F32)


def silu(x):
    half = 0.5 * x
    return half + half * jnp.tanh(half)


def unit_inverses(stricts):
    lane = lax.broadcasted_iota(jnp.int32, (BASE, BLOCK), 1)
    row = lax.broadcasted_iota(jnp.int32, (BASE, BLOCK), 0)
    home = lane // BASE
    count = BLOCK // BASE
    lows = [s.astype(BF16) for s in stricts]
    compact = []
    for s in stricts:
        c = s[0:BASE]
        for b in range(1, count):
            c = jnp.where(home == b, s[b * BASE : (b + 1) * BASE], c)
        compact.append(c)
    eye = jnp.where(lane % BASE == row, 1.0, 0.0).astype(F32)
    xs = [eye for _ in stricts]
    for j in range(BASE - 1):
        index = home * BASE + j
        for n, c in enumerate(compact):
            column = jnp.take_along_axis(c, index, axis=1)
            xs[n] = xs[n] - column * xs[n][j : j + 1]
    slabs = []
    for x in xs:
        slabs.append([jnp.where(home == b, x, 0.0).astype(BF16) for b in range(count)])
    size = BASE
    while size < BLOCK:
        per = size // BASE
        lane_slab = lax.broadcasted_iota(jnp.int32, (size, BLOCK), 1) // size
        odd = [o for o in range(1, BLOCK // size, 2)]
        lefts = [
            jnp.concatenate([slab for o in odd for slab in sl[o * per : (o + 1) * per]], axis=0)
            for sl in slabs
        ]
        wholes = [jnp.concatenate(sl, axis=0) for sl in slabs]
        keep = jnp.concatenate([(lane_slab == o - 1).astype(F32) for o in odd], axis=0) > 0.5
        ys = [jnp.where(keep, dot(a, low), 0.0).astype(BF16) for a, low in zip(lefts, lows)]
        zs = [dot(y, w) for y, w in zip(ys, wholes)]
        for n, z in enumerate(zs):
            new = (lefts[n].astype(F32) - z).astype(BF16)
            for m, o in enumerate(odd):
                for i in range(per):
                    at = m * size + i * BASE
                    slabs[n][o * per + i] = new[at : at + BASE]
        size *= 2
    return [jnp.concatenate(sl, axis=0) for sl in slabs]


def maps_kernel(
    first_ref,
    len_ref,
    qk_ref,
    v_ref,
    rim_ref,
    cqk_ref,
    cv_ref,
    ld_ref,
    wg_ref,
    m_ref,
    out_ref,
    st_ref,
    xqk,
    xv,
    rows,
    gates,
    aq,
    binp,
    base_out,
    carry,
):
    p = pl.program_id(0)
    prompts = pl.num_programs(0)
    tok = v_ref.shape[1]
    nblk = tok // BLOCK
    heads = ld_ref.shape[1]

    xqk[0:RIM, :] = rim_ref[0, 0:RIM, :].astype(F32)
    xqk[RIM:, :] = qk_ref[0].astype(F32)
    for h in range(heads):
        lanes = slice(h * DV, (h + 1) * DV)
        xv[h, 0:RIM, :] = rim_ref[0, (1 + h) * RIM : (2 + h) * RIM, :].astype(F32)
        xv[h, RIM:, :] = v_ref[0, :, lanes].astype(F32)

    position = lax.broadcasted_iota(jnp.int32, (heads, tok), 1) + first_ref[0]
    valid = position < len_ref[p]
    log_gate = jnp.where(valid, ld_ref[0], 0.0)
    gain = jnp.where(valid, wg_ref[0], 0.0)
    rows[...] = jnp.zeros_like(rows)
    for c in range(nblk):
        rows[8 * c : 8 * c + heads, :] = log_gate[:, c * BLOCK : (c + 1) * BLOCK]
        rows[8 * c + heads : 8 * c + 2 * heads, :] = gain[:, c * BLOCK : (c + 1) * BLOCK]
    before = lax.broadcasted_iota(jnp.int32, (BLOCK, BLOCK), 0)
    after = lax.broadcasted_iota(jnp.int32, (BLOCK, BLOCK), 1)
    upto = jnp.where(before <= after, 1.0, 0.0).astype(F32)
    raw_rows = rows[...]
    sums = jnp.dot(raw_rows, upto, precision=lax.Precision.HIGHEST, preferred_element_type=F32)
    kind = lax.broadcasted_iota(jnp.int32, raw_rows.shape, 0) % 8
    rows[...] = jnp.where(kind < heads, sums, raw_rows)

    lower = before >= after
    strictly = before > after
    taps_qk = cqk_ref[...].astype(F32)
    taps_v = cv_ref[...].astype(F32)

    def group(g, _):
        blocks = range(UNROLL)
        queries, keys, keys_t, values, tiles, columns = [], [], [], [], [], []
        for u in blocks:
            c = g * UNROLL + u
            start = c * BLOCK

            def mixed(which):
                total = None
                for i in range(CONV):
                    at = RIM + 2 * (start - (CONV - 1) + i) + which
                    term = xqk[pl.ds(at, BLOCK, stride=2), :] * taps_qk[i, which : which + 1, :]
                    total = term if total is None else total + term
                return silu(total)

            def unit(x):
                return x * lax.rsqrt(jnp.sum(x * x, axis=-1, keepdims=True) + EPSILON)

            q = unit(mixed(0))
            k = unit(mixed(1))
            queries.append(q.astype(BF16))
            keys.append(k.astype(BF16))
            keys_t.append(k.T.astype(BF16))
            vs = []
            for h in range(heads):
                total = None
                for i in range(CONV):
                    at = RIM + start - (CONV - 1) + i
                    term = xv[h, pl.ds(at, BLOCK), :] * taps_v[i : i + 1, h * DV : (h + 1) * DV]
                    total = term if total is None else total + term
                vs.append(silu(total).astype(BF16))
            values.append(vs)
            tile = rows[pl.ds(pl.multiple_of(8 * c, 8), 8), :]
            tiles.append(tile)
            columns.append(tile.T)
        grams = [
            dot(jnp.concatenate([queries[u], keys[u]], axis=0), keys_t[u]) for u in blocks
        ]
        stricts, scores, fades, gains = [], [], [], []
        for u in blocks:
            query_key = grams[u][:BLOCK]
            key_key = jnp.where(strictly, grams[u][BLOCK:], 0.0)
            for h in range(heads):
                cum = jnp.broadcast_to(columns[u][:, h : h + 1], (BLOCK, BLOCK))
                gb = jnp.broadcast_to(columns[u][:, heads + h : heads + h + 1], (BLOCK, BLOCK))
                ratio = jnp.exp(jnp.where(lower, cum - tiles[u][h : h + 1], -1e30))
                stricts.append(ratio * key_key * gb)
                scores.append((ratio * query_key).astype(BF16))
                fades.append(jnp.exp(cum))
                gains.append(gb)
        inverses = unit_inverses(stricts)
        writes = []
        for u in blocks:
            for h in range(heads):
                n = u * heads + h
                scaled_k = (keys[u].astype(F32) * (gains[n] * fades[n])).astype(BF16)
                scaled_v = (values[u][h].astype(F32) * gains[n]).astype(BF16)
                both = jnp.concatenate([scaled_k, scaled_v], axis=1)
                writes.append(dot(inverses[n], both).astype(BF16))
        for u in blocks:
            for h in range(heads):
                n = u * heads + h
                cum_row = tiles[u][h : h + 1]
                last = cum_row[:, BLOCK - 1 : BLOCK]
                tails = (keys_t[u].astype(F32) * jnp.exp(last - cum_row)).astype(BF16)
                r = dot(jnp.concatenate([tails, scores[n]], axis=0), writes[n])
                at = (p * heads + h) * nblk + g * UNROLL + u
                aq[at, 0:DK, :] = (-r[:DK, :DK]).astype(BF16)
                binp[at] = r[:DK, DK:]
                aq[at, DK:, :] = (queries[u].astype(F32) * fades[n] - r[DK:, :DK]).astype(BF16)
                base_out[at] = r[DK:, DK:]
                gates[pl.ds(at, 1), :] = jnp.broadcast_to(jnp.exp(last), (1, BLOCK))
        return 0

    lax.fori_loop(0, nblk // UNROLL, group, 0)

    @pl.when(p == prompts - 1)
    def _():
        chains = carry.shape[0]
        for n in range(chains):
            at = n * nblk
            gate = gates[at : at + 1, :]
            carry[n, :, DK:] = binp[at]
            carry[n, :, :DK] = jnp.where(before == after, gate, 0.0) + aq[at, 0:DK, :].astype(F32)
            m_ref[n, 0:BLOCK, :] = aq[at, DK:, :]
            out_ref[n, 0:BLOCK, :] = base_out[at].astype(BF16)

        def step(c, _):
            for n in range(chains):
                at = n * nblk + c
                state = carry[n]
                r = dot(aq[at], state.astype(BF16))
                gate = gates[pl.ds(at, 1), :]
                carry[n, :, :DK] = gate * state[:, :DK] + r[:DK, :DK]
                carry[n, :, DK:] = gate * state[:, DK:] + r[:DK, DK:] + binp[at]
                tokens = pl.ds(pl.multiple_of(c * BLOCK, BLOCK), BLOCK)
                m_ref[n, tokens, :] = r[DK:, :DK].astype(BF16)
                out_ref[n, tokens, :] = (r[DK:, DK:] + base_out[at]).astype(BF16)
            return 0

        lax.fori_loop(1, nblk, step, 0)
        for n in range(chains):
            st_ref[n % heads, n // heads] = carry[n].astype(BF16)


def local_maps(first, lengths, qk, v, rim, conv_qk, conv_v, log_decay, write_gain):
    prompts, tok = v.shape[:2]
    heads = log_decay.shape[1]
    chains = prompts * heads
    nblk = tok // BLOCK
    units = chains * nblk

    def per_prompt(*shape):
        return pl.BlockSpec((1,) + shape, lambda p: (p,) + (0,) * len(shape))

    def whole(*shape):
        return pl.BlockSpec(shape, lambda p: (0,) * len(shape))

    smem = pl.BlockSpec(memory_space=pltpu.SMEM)
    return pl.pallas_call(
        maps_kernel,
        grid=(prompts,),
        in_specs=[
            smem,
            smem,
            per_prompt(2 * tok, DK),
            per_prompt(tok, heads * DV),
            per_prompt((1 + heads) * RIM, DK),
            whole(*conv_qk.shape),
            whole(*conv_v.shape),
            per_prompt(heads, tok),
            per_prompt(heads, tok),
        ],
        out_specs=[
            whole(chains, tok, DK),
            whole(chains, tok, DV),
            whole(heads, prompts, DK, DK + DV),
        ],
        out_shape=[
            jax.ShapeDtypeStruct((chains, tok, DK), BF16),
            jax.ShapeDtypeStruct((chains, tok, DV), BF16),
            jax.ShapeDtypeStruct((heads, prompts, DK, DK + DV), BF16),
        ],
        scratch_shapes=[
            pltpu.VMEM((RIM + 2 * tok, DK), F32),
            pltpu.VMEM((heads, RIM + tok, DV), F32),
            pltpu.VMEM((8 * nblk, BLOCK), F32),
            pltpu.VMEM((units, BLOCK), F32),
            pltpu.VMEM((units, 2 * BLOCK, DK), BF16),
            pltpu.VMEM((units, DK, DV), F32),
            pltpu.VMEM((units, BLOCK, DV), F32),
            pltpu.VMEM((chains, DK, DK + DV), F32),
        ],
        compiler_params=pltpu.CompilerParams(vmem_limit_bytes=VMEM_LIMIT),
        name="local_maps",
    )(first, lengths, qk, v, rim, conv_qk, conv_v, log_decay, write_gain)


def deliver_kernel(
    len_ref,
    place_ref,
    maps_hbm,
    m_hbm,
    local_hbm,
    z_hbm,
    norm_ref,
    att_hbm,
    roll_hbm,
    maps,
    m,
    local,
    z,
    att,
    pair,
    gathered,
    back,
    got,
    enters,
    finals,
    leaving,
    load_sem,
    store_sem,
    pair_send,
    pair_recv,
    x_send,
    x_recv,
    back_send,
    back_recv,
    head_send,
    head_recv,
    own_sem,
):
    heads, prompts = maps.shape[:2]
    tok = z.shape[1]
    chips = gathered.shape[1]
    s = lax.axis_index("seq")
    row = lax.axis_index("head")
    rows_count = leaving.shape[0]
    core = lax.rem(s, 2)
    chip = lax.div(s, 2)
    mesh_id = pl.DeviceIdType.MESH
    partner = (chip * 2 + 1 - core, row)

    def along_x(d):
        return (lax.rem(chip + d, chips) * 2 + core, row)

    def in_row(d):
        return lax.rem(row + d, rows_count)

    loads = [
        pltpu.make_async_copy(src, dst, load_sem.at[i])
        for i, (src, dst) in enumerate(
            [(maps_hbm, maps), (m_hbm, m), (local_hbm, local), (z_hbm, z)]
        )
    ]
    for load in loads:
        load.start()
    barrier = pltpu.get_barrier_semaphore()
    peers = [partner] + [along_x(d) for d in range(1, chips)]
    peers += [(s, in_row(d)) for d in range(1, rows_count)]
    for peer in peers:
        pl.semaphore_signal(barrier, inc=1, device_id=peer, device_id_type=mesh_id)
    pl.semaphore_wait(barrier, len(peers))

    loads[0].wait()
    swaps = []
    for p in range(prompts):
        swap = pltpu.make_async_remote_copy(
            maps.at[1 - core, p],
            pair.at[p],
            pair_send.at[p],
            pair_recv.at[p],
            device_id=partner,
            device_id_type=mesh_id,
        )
        swap.start()
        swaps.append(swap)
    spreads = []
    for p in range(prompts):
        swaps[p].wait_recv()
        own = maps[core, p]
        other = pair[p]
        early = jnp.where(core == 0, own, other)
        late = jnp.where(core == 0, other, own)
        both = dot(late[:, :DK], early)
        joined = jnp.concatenate(
            [both[:, :DK], both[:, DK:] + late[:, DK:].astype(F32)], axis=1
        )
        gathered[p, chip] = joined.astype(BF16)
        for d in range(1, chips):
            spread = pltpu.make_async_remote_copy(
                gathered.at[p, chip],
                gathered.at[p, chip],
                x_send.at[p, d - 1],
                x_recv.at[p, d - 1],
                device_id=along_x(d),
                device_id_type=mesh_id,
            )
            spread.start()
            spreads.append(spread)
    returns = []
    for p in range(prompts):
        for d in range(1, chips):
            spreads[p * (chips - 1) + d - 1].wait_recv()
        state = jnp.zeros((DK, DV), F32)
        enter = state
        for k in range(chips):
            enter = jnp.where(chip == k, state, enter)
            tk = gathered[p, k]
            if k == 0:
                state = tk[:, DK:].astype(F32)
            else:
                state = dot(tk[:, :DK], state.astype(BF16)) + tk[:, DK:].astype(F32)
        first_map = jnp.where(core == 0, maps[core, p], pair[p])
        enter = enter.astype(BF16)
        second = (dot(first_map[:, :DK], enter) + first_map[:, DK:].astype(F32)).astype(BF16)
        final = state.astype(BF16)
        finals[core, p] = final
        enters[core, p] = jnp.where(core == 0, enter, second)
        back[p, 0] = jnp.where(core == 0, second, enter)
        back[p, 1] = final
        ret = pltpu.make_async_remote_copy(
            back.at[p],
            got.at[p],
            back_send.at[p],
            back_recv.at[p],
            device_id=partner,
            device_id_type=mesh_id,
        )
        ret.start()
        returns.append(ret)
    for p in range(prompts):
        returns[p].wait_recv()
        enters[1 - core, p] = got[p, 0]
        finals[1 - core, p] = got[p, 1]
    sends = []
    for d in range(1, rows_count):
        to = in_row(d)
        chosen = place_ref[0, to]
        for h in range(heads):
            leaving[d, h] = finals[h, chosen]
        send = pltpu.make_async_remote_copy(
            leaving.at[d],
            roll_hbm.at[row],
            head_send.at[d],
            head_recv.at[d],
            device_id=(s, to),
            device_id_type=mesh_id,
        )
        send.start()
        sends.append(send)
    chosen = place_ref[0, row]
    for h in range(heads):
        leaving[0, h] = finals[h, chosen]
    keep = pltpu.make_async_copy(leaving.at[0], roll_hbm.at[row], own_sem)
    keep.start()

    for load in loads[1:]:
        load.wait()
    norm_gain = norm_ref[...]
    step = 128

    def prompt(p, _):
        length = len_ref[p]

        def tokens(i, _):
            at = pl.ds(pl.multiple_of(i * step, step), step)
            position = s * tok + i * step + lax.broadcasted_iota(jnp.int32, (step, DV), 0)
            valid = position < length
            for h in range(heads):
                n = p * heads + h
                raw = dot(m[n, at, :], enters[h, p]) + local[n, at, :].astype(F32)
                scaled = raw * lax.rsqrt(jnp.mean(raw * raw, axis=-1, keepdims=True) + EPSILON)
                zh = z[p, at, h * DV : (h + 1) * DV].astype(F32)
                gated = scaled * norm_gain * silu(zh)
                att[p, at, h * DV : (h + 1) * DV] = jnp.where(valid, gated, 0.0).astype(BF16)
            return 0

        lax.fori_loop(0, tok // step, tokens, 0, unroll=2)
        return 0

    lax.fori_loop(0, prompts, prompt, 0)
    store = pltpu.make_async_copy(att, att_hbm, store_sem)
    store.start()
    for copy in swaps + spreads + returns:
        copy.wait_send()
    for send in sends:
        send.wait()
    keep.wait()
    store.wait()


def deliver(lengths, placement, maps, m, local, gate_z, norm_gain, chips, rows_count):
    prompts, tok, width = gate_z.shape
    heads = maps.shape[0]
    smem = pl.BlockSpec(memory_space=pltpu.SMEM)
    hbm = pl.BlockSpec(memory_space=pl.ANY)
    vmem = pl.BlockSpec(memory_space=pltpu.VMEM)
    dma = pltpu.SemaphoreType.DMA
    return pl.pallas_call(
        deliver_kernel,
        in_specs=[smem, smem, hbm, hbm, hbm, hbm, vmem],
        out_specs=[hbm, hbm],
        out_shape=[
            jax.ShapeDtypeStruct((prompts, tok, width), BF16),
            jax.ShapeDtypeStruct((rows_count, heads, DK, DV), BF16),
        ],
        scratch_shapes=[
            pltpu.VMEM(maps.shape, BF16),
            pltpu.VMEM(m.shape, BF16),
            pltpu.VMEM(local.shape, BF16),
            pltpu.VMEM(gate_z.shape, BF16),
            pltpu.VMEM(gate_z.shape, BF16),
            pltpu.VMEM((prompts, DK, DK + DV), BF16),
            pltpu.VMEM((prompts, chips, DK, DK + DV), BF16),
            pltpu.VMEM((prompts, 2, DK, DV), BF16),
            pltpu.VMEM((prompts, 2, DK, DV), BF16),
            pltpu.VMEM((heads, prompts, DK, DV), BF16),
            pltpu.VMEM((heads, prompts, DK, DV), BF16),
            pltpu.VMEM((rows_count, heads, DK, DV), BF16),
            dma((4,)),
            dma,
            dma((prompts,)),
            dma((prompts,)),
            dma((prompts, chips - 1)),
            dma((prompts, chips - 1)),
            dma((prompts,)),
            dma((prompts,)),
            dma((rows_count,)),
            dma((rows_count,)),
            dma,
        ],
        compiler_params=pltpu.CompilerParams(
            vmem_limit_bytes=VMEM_LIMIT, collective_id=0, has_side_effects=True
        ),
        name="deliver",
    )(lengths, placement, maps, m, local, gate_z, norm_gain)


def shards(
    qk_in,
    v_in,
    gate_z,
    conv_qk,
    conv_v,
    log_decay,
    write_gain,
    norm_gain,
    prompt_lengths,
    placement,
):
    prompts, tok = v_in.shape[:2]
    heads = log_decay.shape[1]
    head_count = lax.axis_size("head")
    seq_count = lax.axis_size("seq")
    qk = qk_in.reshape(prompts, 2 * tok, DK)
    tails = jnp.concatenate(
        [qk[:, 2 * tok - RIM :]]
        + [v_in[:, tok - RIM :, h * DV : (h + 1) * DV] for h in range(heads)],
        axis=1,
    )
    rim = lax.ppermute(tails, "seq", [(i, i + 1) for i in range(seq_count - 1)])
    first = (lax.axis_index("seq") * tok).astype(jnp.int32).reshape(1)
    m, local, st = local_maps(
        first, prompt_lengths, qk, v_in, rim, conv_qk, conv_v, log_decay, write_gain
    )
    attended, arrived = deliver(
        prompt_lengths,
        placement,
        st,
        m,
        local,
        gate_z,
        norm_gain.reshape(1, DV),
        seq_count // 2,
        head_count,
    )
    rollout = arrived.astype(F32).reshape(1, 1, head_count * heads, DK, DV)
    return attended, rollout


def solution(mesh):
    return jax.shard_map(
        shards,
        mesh=mesh,
        in_specs=(
            P(None, "seq", None, "head"),
            P(None, "seq", "head"),
            P(None, "seq", "head"),
            P(None, None, "head"),
            P(None, "head"),
            P(None, "head", "seq"),
            P(None, "head", "seq"),
            P(),
            P(),
            P("seq", None),
        ),
        out_specs=(P(None, "seq", "head"), P("seq", "head", None, None, None)),
        check_vma=False,
    )
```

```python
import functools

import jax
import jax.numpy as jnp
from jax import lax
from jax.experimental import pallas as pl
from jax.experimental.pallas import tpu as pltpu
from jax.sharding import PartitionSpec as P

DK = 128
DV = 128
CONV = 4
BLOCK = 128
BASE = 16
UNROLL = 4
RIM = 16
EPSILON = 1e-06
F32 = jnp.float32
BF16 = jnp.bfloat16
VMEM_LIMIT = 56 * 1024 * 1024


def dot(a, b):
    return jnp.dot(a, b, preferred_element_type=F32)


def silu(x):
    half = 0.5 * x
    return half + half * jnp.tanh(half)


def base_inverses(stricts):
    half = BASE // 2
    lane = lax.broadcasted_iota(jnp.int32, (half, BLOCK), 1)
    row = lax.broadcasted_iota(jnp.int32, (half, BLOCK), 0)
    home = lane // BASE
    tops, bots, lows_top, lows_bot = [], [], [], []
    for s in stricts:
        top, bot = s[0:half], s[half:BASE]
        for b in range(1, BLOCK // BASE):
            top = jnp.where(home == b, s[b * BASE : b * BASE + half], top)
            bot = jnp.where(home == b, s[b * BASE + half : (b + 1) * BASE], bot)
        lows_top.append(top)
        lows_bot.append(bot)
        tops.append(jnp.where(lane % BASE == row, 1.0, 0.0).astype(F32))
        bots.append(jnp.where(lane % BASE == row + half, 1.0, 0.0).astype(F32))
    for j in range(BASE - 1):
        index = home * BASE + j
        for n in range(len(stricts)):
            source = tops[n][j : j + 1] if j < half else bots[n][j - half : j - half + 1]
            if j < half - 1:
                tops[n] = tops[n] - jnp.take_along_axis(lows_top[n], index, axis=1) * source
            bots[n] = bots[n] - jnp.take_along_axis(lows_bot[n], index, axis=1) * source
    return [jnp.concatenate([t, b], axis=0) for t, b in zip(tops, bots)]


def merge_levels(slabs, lows):
    size = BASE
    while size < BLOCK // 2:
        per = size // BASE
        lane_slab = lax.broadcasted_iota(jnp.int32, (size, BLOCK), 1) // size
        odd = [o for o in range(1, BLOCK // size, 2)]
        lefts = [
            jnp.concatenate([slab for o in odd for slab in sl[o * per : (o + 1) * per]], axis=0)
            for sl in slabs
        ]
        wholes = [jnp.concatenate(sl, axis=0) for sl in slabs]
        keep = jnp.concatenate([(lane_slab == o - 1).astype(F32) for o in odd], axis=0) > 0.5
        ys = [jnp.where(keep, dot(a, low), 0.0).astype(BF16) for a, low in zip(lefts, lows)]
        zs = [dot(y, w) for y, w in zip(ys, wholes)]
        for n, z in enumerate(zs):
            new = (lefts[n].astype(F32) - z).astype(BF16)
            for m, o in enumerate(odd):
                for i in range(per):
                    at = m * size + i * BASE
                    slabs[n][o * per + i] = new[at : at + BASE]
        size *= 2


def delta_kernel(
    len_ref,
    place_ref,
    qk_hbm,
    v_hbm,
    z_hbm,
    cqk_ref,
    cv_ref,
    ld_ref,
    wg_ref,
    norm_ref,
    att_hbm,
    roll_hbm,
    qk,
    v,
    z,
    att,
    rim_qk,
    rim_v,
    xqk,
    xv,
    rows,
    m,
    local,
    carry,
    strict_a,
    strict_b,
    base_a,
    base_b,
    left_a,
    left_b,
    both_a,
    both_b,
    fadeq_a,
    fadeq_b,
    gate_a,
    gate_b,
    aq_0,
    aq_1,
    binp_0,
    binp_1,
    bout_0,
    bout_1,
    step_0,
    step_1,
    maps,
    pair,
    gathered,
    back,
    got,
    enters,
    finals,
    leaving,
    qk_sem,
    v_sem,
    z_sem,
    store_sem,
    rim_send,
    rim_recv,
    pair_send,
    pair_recv,
    x_send,
    x_recv,
    back_send,
    back_recv,
    head_send,
    head_recv,
    own_sem,
):
    prompts, tok = v.shape[:2]
    heads = ld_ref.shape[1]
    nblk = tok // BLOCK
    half_tok = UNROLL * BLOCK
    chips = gathered.shape[1]
    rows_count = leaving.shape[0]
    seq_count = 2 * chips
    s = lax.axis_index("seq")
    row = lax.axis_index("head")
    core = lax.rem(s, 2)
    chip = lax.div(s, 2)
    mesh_id = pl.DeviceIdType.MESH
    partner = (chip * 2 + 1 - core, row)
    following = (lax.rem(s + 1, seq_count), row)
    preceding = (lax.rem(s + seq_count - 1, seq_count), row)
    sets = {
        1: (strict_b, base_b, left_b, both_b, fadeq_b, gate_b),
        0: (strict_a, base_a, left_a, both_a, fadeq_a, gate_a),
    }

    def results(p, half):
        if half == 0:
            return aq_0, binp_0, bout_0, step_0
        return [ref.at[lax.rem(p, 2)] for ref in (aq_1, binp_1, bout_1, step_1)]

    def along_x(d):
        return (lax.rem(chip + d, chips) * 2 + core, row)

    def in_row(d):
        return lax.rem(row + d, rows_count)

    def load_qk(p):
        return pltpu.make_async_copy(qk_hbm.at[p], qk.at[p], qk_sem.at[p])

    def load_v(p):
        return pltpu.make_async_copy(v_hbm.at[p], v.at[p], v_sem.at[p])

    load_z = pltpu.make_async_copy(z_hbm, z, z_sem)
    for p in range(prompts):
        load_qk(p).start()
        load_v(p).start()
    load_z.start()
    barrier = pltpu.get_barrier_semaphore()
    peers = [following, preceding]
    peers += [along_x(d) for d in range(1, chips)]
    peers += [(s, in_row(d)) for d in range(1, rows_count)]
    for peer in peers:
        pl.semaphore_signal(barrier, inc=1, device_id=peer, device_id_type=mesh_id)

    before = lax.broadcasted_iota(jnp.int32, (BLOCK, BLOCK), 0)
    after = lax.broadcasted_iota(jnp.int32, (BLOCK, BLOCK), 1)
    lower = before >= after
    strictly = before > after
    upto = jnp.where(before <= after, 1.0, 0.0).astype(F32)
    rows[...] = jnp.zeros_like(rows)
    position = lax.broadcasted_iota(jnp.int32, (heads, tok), 1) + s * tok
    for p in range(prompts):
        valid = position < len_ref[p]
        log_gate = jnp.where(valid, ld_ref[p], 0.0)
        gain = jnp.where(valid, wg_ref[p], 0.0)
        for c in range(nblk):
            at = 8 * (p * nblk + c)
            rows[at : at + heads, :] = log_gate[:, c * BLOCK : (c + 1) * BLOCK]
            rows[at + heads : at + 2 * heads, :] = gain[:, c * BLOCK : (c + 1) * BLOCK]
    raw_rows = rows[...]
    sums = jnp.dot(raw_rows, upto, precision=lax.Precision.HIGHEST, preferred_element_type=F32)
    kind = lax.broadcasted_iota(jnp.int32, raw_rows.shape, 0) % 8
    rows[...] = jnp.where(kind < heads, sums, raw_rows)
    taps_qk = cqk_ref[...].astype(F32)
    taps_v = cv_ref[...].astype(F32)

    def prepare(p, half):
        strict_ref, base_ref, left_ref, both_ref, fadeq_ref, gate_ref = sets[half]
        blocks = range(UNROLL)
        start = half * half_tok
        if half == 0:
            scale = jnp.where(s == 0, 0.0, 1.0).astype(F32)
            xqk[0:RIM, :] = rim_qk[p].astype(F32) * scale
        else:
            xqk[0:RIM, :] = qk[p, 2 * start - RIM : 2 * start, :].astype(F32)
        xqk[RIM:, :] = qk[p, 2 * start : 2 * (start + half_tok), :].astype(F32)
        for h in range(heads):
            lanes = slice(h * DV, (h + 1) * DV)
            if half == 0:
                xv[h, 0:RIM, :] = rim_v[p, :, lanes].astype(F32) * scale
            else:
                xv[h, 0:RIM, :] = v[p, start - RIM : start, lanes].astype(F32)
            xv[h, RIM:, :] = v[p, start : start + half_tok, lanes].astype(F32)

        def mixed(u, which):
            total = None
            for i in range(CONV):
                at = RIM + 2 * (u * BLOCK - (CONV - 1) + i) + which
                term = xqk[pl.ds(at, BLOCK, stride=2), :] * taps_qk[i, which : which + 1, :]
                total = term if total is None else total + term
            return silu(total)

        def unit(x):
            return x * lax.rsqrt(jnp.sum(x * x, axis=-1, keepdims=True) + EPSILON)

        queries, keys, keys_t, values, tiles, columns = [], [], [], [], [], []
        for u in blocks:
            q = unit(mixed(u, 0))
            k = unit(mixed(u, 1))
            queries.append(q.astype(BF16))
            keys.append(k.astype(BF16))
            keys_t.append(k.T.astype(BF16))
            vs = []
            for h in range(heads):
                total = None
                for i in range(CONV):
                    at = RIM + u * BLOCK - (CONV - 1) + i
                    term = xv[h, at : at + BLOCK, :] * taps_v[i : i + 1, h * DV : (h + 1) * DV]
                    total = term if total is None else total + term
                vs.append(silu(total).astype(BF16))
            values.append(vs)
            at = pl.multiple_of(8 * (p * nblk + half * UNROLL + u), 8)
            tile = rows[pl.ds(at, 8), :]
            tiles.append(tile)
            columns.append(tile.T)
        grams = [dot(jnp.concatenate([queries[u], keys[u]], axis=0), keys_t[u]) for u in blocks]
        stricts = []
        for u in blocks:
            query_key = grams[u][:BLOCK]
            key_key = jnp.where(strictly, grams[u][BLOCK:], 0.0)
            for h in range(heads):
                n = u * heads + h
                cum_row = tiles[u][h : h + 1]
                last = cum_row[:, BLOCK - 1 : BLOCK]
                cum = jnp.broadcast_to(columns[u][:, h : h + 1], (BLOCK, BLOCK))
                gb = jnp.broadcast_to(columns[u][:, heads + h : heads + h + 1], (BLOCK, BLOCK))
                ratio = jnp.exp(jnp.where(lower, cum - cum_row, -1e30))
                fade = jnp.exp(cum)
                strict = ratio * key_key * gb
                stricts.append(strict)
                strict_ref[n] = strict.astype(BF16)
                left_ref[n, 0:DK, :] = (
                    keys_t[u].astype(F32) * jnp.exp(last - cum_row)
                ).astype(BF16)
                left_ref[n, DK:, :] = (ratio * query_key).astype(BF16)
                both_ref[n, :, 0:DK] = (keys[u].astype(F32) * (gb * fade)).astype(BF16)
                both_ref[n, :, DK:] = (values[u][h].astype(F32) * gb).astype(BF16)
                fadeq_ref[n] = queries[u].astype(F32) * fade
                gate_ref[n : n + 1, :] = jnp.broadcast_to(jnp.exp(last), (1, BLOCK))
        for n, x in enumerate(base_inverses(stricts)):
            base_ref[n] = x

    def solve(p, half):
        strict_ref, base_ref, left_ref, both_ref, fadeq_ref, gate_ref = sets[half]
        aq, binp, bout, step = results(p, half)
        units = range(UNROLL * heads)
        mid = BLOCK // 2
        home = lax.broadcasted_iota(jnp.int32, (BASE, BLOCK), 1) // BASE
        lows = [strict_ref[n] for n in units]
        slabs = []
        for n in units:
            x = base_ref[n]
            slabs.append(
                [jnp.where(home == b, x, 0.0).astype(BF16) for b in range(BLOCK // BASE)]
            )
        merge_levels(slabs, lows)
        per = mid // BASE
        tops = [jnp.concatenate(sl[:per], axis=0)[:, :mid] for sl in slabs]
        bots = [jnp.concatenate(sl[per:], axis=0)[:, mid:] for sl in slabs]
        w1 = [dot(tops[n], both_ref[n, 0:mid, :]).astype(BF16) for n in units]
        rest = [
            (both_ref[n, mid:, :].astype(F32) - dot(lows[n][mid:, :mid], w1[n])).astype(BF16)
            for n in units
        ]
        w2 = [dot(bots[n], rest[n]).astype(BF16) for n in units]
        for n in units:
            r = dot(left_ref[n], jnp.concatenate([w1[n], w2[n]], axis=0))
            aq[n, 0:DK, :] = (-r[:DK, :DK]).astype(BF16)
            binp[n] = r[:DK, DK:]
            aq[n, DK:, :] = (fadeq_ref[n] - r[DK:, :DK]).astype(BF16)
            bout[n] = r[DK:, DK:]
        step[...] = gate_ref[...]

    def advance(p, half):
        aq, binp, bout, step = results(p, half)
        states = [carry[h] for h in range(heads)]
        for u in range(UNROLL):
            tokens = slice(half * half_tok + u * BLOCK, half * half_tok + (u + 1) * BLOCK)
            for h in range(heads):
                n = u * heads + h
                gate = step[n : n + 1, :]
                chain = p * heads + h
                if half == 0 and u == 0:
                    trans = jnp.where(before == after, gate, 0.0) + aq[n, 0:DK, :].astype(F32)
                    states[h] = jnp.concatenate([trans, binp[n]], axis=1)
                    m[chain, tokens, :] = aq[n, DK:, :]
                    local[chain, tokens, :] = bout[n].astype(BF16)
                    continue
                r = dot(aq[n], states[h].astype(BF16))
                wide = jnp.concatenate([gate, gate], axis=1)
                inputs = jnp.concatenate([jnp.zeros((DK, DK), F32), binp[n]], axis=1)
                states[h] = wide * states[h] + r[:DK] + inputs
                m[chain, tokens, :] = r[DK:, :DK].astype(BF16)
                local[chain, tokens, :] = (r[DK:, DK:] + bout[n]).astype(BF16)
        for h in range(heads):
            if half == 0:
                carry[h] = states[h]
            else:
                maps[h, p] = states[h].astype(BF16)

    def swap(p):
        return pltpu.make_async_remote_copy(
            maps.at[1 - core, p],
            pair.at[p],
            pair_send.at[p],
            pair_recv.at[p],
            device_id=partner,
            device_id_type=mesh_id,
        )

    def spread(p, d):
        return pltpu.make_async_remote_copy(
            gathered.at[p, chip],
            gathered.at[p, chip],
            x_send.at[p, d - 1],
            x_recv.at[p, d - 1],
            device_id=along_x(d),
            device_id_type=mesh_id,
        )

    def give_back(p):
        return pltpu.make_async_remote_copy(
            back.at[p],
            got.at[p],
            back_send.at[p],
            back_recv.at[p],
            device_id=partner,
            device_id_type=mesh_id,
        )

    def join_pair(p):
        swap(p).wait_recv()
        own = maps[core, p]
        other = pair[p]
        early = jnp.where(core == 0, own, other)
        late = jnp.where(core == 0, other, own)
        both = dot(late[:, :DK], early)
        joined = jnp.concatenate([both[:, :DK], both[:, DK:] + late[:, DK:].astype(F32)], axis=1)
        gathered[p, chip] = joined.astype(BF16)
        for d in range(1, chips):
            spread(p, d).start()

    def compose(p):
        for d in range(1, chips):
            spread(p, d).wait_recv()
        state = gathered[p, 0][:, DK:].astype(F32)
        enter = jnp.where(chip == 1, state, 0.0)
        for k in range(1, chips):
            tk = gathered[p, k]
            state = dot(tk[:, :DK], state.astype(BF16)) + tk[:, DK:].astype(F32)
            if k < chips - 1:
                enter = jnp.where(chip == k + 1, state, enter)
        first_map = jnp.where(core == 0, maps[core, p], pair[p])
        enter = enter.astype(BF16)
        second = (dot(first_map[:, :DK], enter) + first_map[:, DK:].astype(F32)).astype(BF16)
        final = state.astype(BF16)
        finals[core, p] = final
        enters[core, p] = jnp.where(core == 0, enter, second)
        back[p, 0] = jnp.where(core == 0, second, enter)
        back[p, 1] = final
        give_back(p).start()

    def receive(p):
        give_back(p).wait_recv()
        enters[1 - core, p] = got[p, 0]
        finals[1 - core, p] = got[p, 1]

    norm_gain = norm_ref[...]
    stride = 128

    def finish(p):
        length = len_ref[p]

        def tokens(i, _):
            at = pl.ds(pl.multiple_of(i * stride, stride), stride)
            place = s * tok + i * stride + lax.broadcasted_iota(jnp.int32, (stride, DV), 0)
            valid = place < length
            for h in range(heads):
                n = p * heads + h
                raw = dot(m[n, at, :], enters[h, p]) + local[n, at, :].astype(F32)
                scaled = raw * lax.rsqrt(jnp.mean(raw * raw, axis=-1, keepdims=True) + EPSILON)
                zh = z[p, at, h * DV : (h + 1) * DV].astype(F32)
                gated = scaled * norm_gain * silu(zh)
                att[p, at, h * DV : (h + 1) * DV] = jnp.where(valid, gated, 0.0).astype(BF16)
            return 0

        lax.fori_loop(0, tok // stride, tokens, 0, unroll=2)

    load_qk(0).wait()
    load_v(0).wait()
    prepare(0, 1)
    pl.semaphore_wait(barrier, len(peers))
    rims = [
        pltpu.make_async_remote_copy(
            src.at[:, pl.ds(src.shape[1] - RIM, RIM), :],
            dst,
            rim_send.at[i],
            rim_recv.at[i],
            device_id=following,
            device_id_type=mesh_id,
        )
        for i, (src, dst) in enumerate([(qk_hbm, rim_qk), (v_hbm, rim_v)])
    ]
    for rim in rims:
        rim.start()
    for rim in rims:
        rim.wait()

    def prompt(p, _):
        earlier = jnp.maximum(p - 1, 0)
        later = jnp.minimum(p + 1, prompts - 1)
        solve(p, 1)
        prepare(p, 0)
        advance(earlier, 0)

        @pl.when(p < prompts - 1)
        def _():
            load_qk(p + 1).wait()
            load_v(p + 1).wait()

        @pl.when(p >= 2)
        def _():
            join_pair(p - 2)

        solve(p, 0)
        prepare(later, 1)
        advance(earlier, 1)

        @pl.when(p >= 1)
        def _():
            swap(p - 1).start()

        return 0

    lax.fori_loop(0, prompts, prompt, 0)
    last = prompts - 1
    join_pair(last - 1)
    advance(last, 0)
    advance(last, 1)
    swap(last).start()
    for p in range(last - 1):
        compose(p)
    join_pair(last)
    load_z.wait()
    for p in range(last - 1):
        receive(p)
        finish(p)
    compose(last - 1)
    compose(last)
    receive(last - 1)
    receive(last)
    sends = []
    for d in range(1, rows_count):
        to = in_row(d)
        chosen = place_ref[0, to]
        for h in range(heads):
            leaving[d, h] = finals[h, chosen]
        send = pltpu.make_async_remote_copy(
            leaving.at[d],
            roll_hbm.at[row],
            head_send.at[d],
            head_recv.at[d],
            device_id=(s, to),
            device_id_type=mesh_id,
        )
        send.start()
        sends.append(send)
    chosen = place_ref[0, row]
    for h in range(heads):
        leaving[0, h] = finals[h, chosen]
    keep = pltpu.make_async_copy(leaving.at[0], roll_hbm.at[row], own_sem)
    keep.start()
    finish(last - 1)
    finish(last)
    store = pltpu.make_async_copy(att, att_hbm, store_sem)
    store.start()
    for p in range(prompts):
        swap(p).wait_send()
        for d in range(1, chips):
            spread(p, d).wait_send()
        give_back(p).wait_send()
    for send in sends:
        send.wait()
    keep.wait()
    store.wait()


def delta(lengths, placement, qk, v, z, conv_qk, conv_v, log_decay, write_gain, norm_gain, chips, rows_count):
    prompts, tok, width = v.shape
    heads = width // DV
    chains = prompts * heads
    units = UNROLL * heads
    nblk = tok // BLOCK
    smem = pl.BlockSpec(memory_space=pltpu.SMEM)
    hbm = pl.BlockSpec(memory_space=pl.ANY)
    vmem = pl.BlockSpec(memory_space=pltpu.VMEM)
    dma = pltpu.SemaphoreType.DMA

    def twice(*spec):
        return [pltpu.VMEM(*spec), pltpu.VMEM(*spec)]

    return pl.pallas_call(
        delta_kernel,
        in_specs=[smem, smem, hbm, hbm, hbm, vmem, vmem, vmem, vmem, vmem],
        out_specs=[hbm, hbm],
        out_shape=[
            jax.ShapeDtypeStruct((prompts, tok, width), BF16),
            jax.ShapeDtypeStruct((rows_count, heads, DK, DV), BF16),
        ],
        scratch_shapes=[
            pltpu.VMEM(qk.shape, BF16),
            pltpu.VMEM(v.shape, BF16),
            pltpu.VMEM(z.shape, BF16),
            pltpu.VMEM(z.shape, BF16),
            pltpu.VMEM((prompts, RIM, DK), BF16),
            pltpu.VMEM((prompts, RIM, width), BF16),
            pltpu.VMEM((RIM + 2 * UNROLL * BLOCK, DK), F32),
            pltpu.VMEM((heads, RIM + UNROLL * BLOCK, DV), F32),
            pltpu.VMEM((8 * prompts * nblk, BLOCK), F32),
            pltpu.VMEM((chains, tok, DK), BF16),
            pltpu.VMEM((chains, tok, DV), BF16),
            pltpu.VMEM((heads, DK, DK + DV), F32),
            *twice((units, BLOCK, BLOCK), BF16),
            *twice((units, BASE, BLOCK), F32),
            *twice((units, 2 * BLOCK, BLOCK), BF16),
            *twice((units, BLOCK, DK + DV), BF16),
            *twice((units, BLOCK, DK), F32),
            *twice((units, BLOCK), F32),
            pltpu.VMEM((units, 2 * BLOCK, DK), BF16),
            pltpu.VMEM((2, units, 2 * BLOCK, DK), BF16),
            pltpu.VMEM((units, DK, DV), F32),
            pltpu.VMEM((2, units, DK, DV), F32),
            pltpu.VMEM((units, BLOCK, DV), F32),
            pltpu.VMEM((2, units, BLOCK, DV), F32),
            pltpu.VMEM((units, BLOCK), F32),
            pltpu.VMEM((2, units, BLOCK), F32),
            pltpu.VMEM((heads, prompts, DK, DK + DV), BF16),
            pltpu.VMEM((prompts, DK, DK + DV), BF16),
            pltpu.VMEM((prompts, chips, DK, DK + DV), BF16),
            pltpu.VMEM((prompts, 2, DK, DV), BF16),
            pltpu.VMEM((prompts, 2, DK, DV), BF16),
            pltpu.VMEM((heads, prompts, DK, DV), BF16),
            pltpu.VMEM((heads, prompts, DK, DV), BF16),
            pltpu.VMEM((rows_count, heads, DK, DV), BF16),
            dma((prompts,)),
            dma((prompts,)),
            dma,
            dma,
            dma((2,)),
            dma((2,)),
            dma((prompts,)),
            dma((prompts,)),
            dma((prompts, chips - 1)),
            dma((prompts, chips - 1)),
            dma((prompts,)),
            dma((prompts,)),
            dma((rows_count,)),
            dma((rows_count,)),
            dma,
        ],
        compiler_params=pltpu.CompilerParams(
            vmem_limit_bytes=VMEM_LIMIT, collective_id=0, has_side_effects=True
        ),
        name="delta",
    )(lengths, placement, qk, v, z, conv_qk, conv_v, log_decay, write_gain, norm_gain)


def shards(
    qk_in,
    v_in,
    gate_z,
    conv_qk,
    conv_v,
    log_decay,
    write_gain,
    norm_gain,
    prompt_lengths,
    placement,
):
    prompts, tok = v_in.shape[:2]
    heads = log_decay.shape[1]
    head_count = lax.axis_size("head")
    seq_count = lax.axis_size("seq")
    attended, arrived = delta(
        prompt_lengths,
        placement,
        qk_in.reshape(prompts, 2 * tok, DK),
        v_in,
        gate_z,
        conv_qk,
        conv_v,
        log_decay,
        write_gain,
        norm_gain.reshape(1, DV),
        seq_count // 2,
        head_count,
    )
    rollout = arrived.astype(F32).reshape(1, 1, head_count * heads, DK, DV)
    return attended, rollout


def solution(mesh):
    return jax.shard_map(
        shards,
        mesh=mesh,
        in_specs=(
            P(None, "seq", None, "head"),
            P(None, "seq", "head"),
            P(None, "seq", "head"),
            P(None, None, "head"),
            P(None, "head"),
            P(None, "head", "seq"),
            P(None, "head", "seq"),
            P(),
            P(),
            P("seq", None),
        ),
        out_specs=(P(None, "seq", "head"), P("seq", "head", None, None, None)),
        check_vma=False,
    )
```

```python
import functools

import jax
import jax.numpy as jnp
from jax import lax
from jax.experimental import pallas as pl
from jax.experimental.pallas import tpu as pltpu
from jax.sharding import PartitionSpec as P

DK = 128
DV = 128
CONV = 4
BLOCK = 128
BASE = 16
UNROLL = 4
RIM = 16
EPSILON = 1e-06
LOG2E = 1.4426950408889634
F32 = jnp.float32
BF16 = jnp.bfloat16
VMEM_LIMIT = 28 * 1024 * 1024


def dot(a, b):
    return jnp.dot(a, b, preferred_element_type=F32)


def silu_of_twice(half):
    return half + half * jnp.tanh(half)


def silu(x):
    return silu_of_twice(0.5 * x)


def interleave(*parts):
    parts = [[0, count, steps] for steps, count in parts]
    while parts:
        part = min(parts, key=lambda p: p[0] / p[1])
        part[0] += 1
        try:
            next(part[2])
        except StopIteration:
            parts.remove(part)


def base_inverses(stricts, masks):
    half = BASE // 2
    lane = lax.broadcasted_iota(jnp.int32, (half, BLOCK), 1)
    row = lax.broadcasted_iota(jnp.int32, (half, BLOCK), 0)
    home = lane // BASE
    tops, bots, lows_top, lows_bot = [], [], [], []
    for s in stricts:
        compact = s[0:BASE] * masks[0]
        for b in range(1, BLOCK // BASE):
            compact = compact + s[b * BASE : (b + 1) * BASE] * masks[b]
        compact = compact.astype(F32)
        lows_top.append(compact[:half])
        lows_bot.append(compact[half:])
        tops.append(jnp.where(lane % BASE == row, 1.0, 0.0).astype(F32))
        bots.append(jnp.where(lane % BASE == row + half, 1.0, 0.0).astype(F32))
    yield
    for j in range(BASE - 1):
        index = home * BASE + j
        for n in range(len(stricts)):
            source = tops[n][j : j + 1] if j < half else bots[n][j - half : j - half + 1]
            if j < half - 1:
                tops[n] = tops[n] - jnp.take_along_axis(lows_top[n], index, axis=1) * source
            bots[n] = bots[n] - jnp.take_along_axis(lows_bot[n], index, axis=1) * source
        yield
    return [jnp.concatenate([t, b], axis=0) for t, b in zip(tops, bots)]


def lane_masks(size):
    home = lax.broadcasted_iota(jnp.int32, (size, BLOCK), 1) // size
    return [jnp.where(home == b, 1.0, 0.0).astype(BF16) for b in range(BLOCK // size)]


def stacked_products(lefts, rights):
    out = []
    for n in range(0, len(lefts), 2):
        size = lefts[n].shape[0]
        both = dot(
            jnp.concatenate(lefts[n : n + 2], axis=0), jnp.concatenate(rights[n : n + 2], axis=1)
        )
        out += [both[:size, :BLOCK].astype(BF16), both[size:, BLOCK:].astype(BF16)]
        yield
    return out


def merge_blocks(inverses, lows):
    size = BASE
    while size < BLOCK // 2:
        masks = lane_masks(size)
        count = BLOCK // size
        evens = sum(masks[2::2], masks[0])
        odds = sum(masks[3::2], masks[1])
        zeros = jnp.zeros((size, BLOCK), BF16)
        below = [
            jnp.concatenate(
                [
                    low[o * size : (o + 1) * size] * masks[o - 1] if o % 2 else zeros
                    for o in range(count)
                ],
                axis=0,
            )
            for low in lows
        ]
        above = [
            jnp.concatenate([zeros if e % 2 else x * masks[e] for e in range(count)], axis=0)
            for x in inverses
        ]
        ys = yield from stacked_products(inverses, below)
        zs = yield from stacked_products(ys, above)
        inverses = [
            jnp.concatenate([x * evens, x * odds - z], axis=0) for x, z in zip(inverses, zs)
        ]
        size *= 2
    return inverses


def delta_kernel(
    len_hbm,
    place_hbm,
    qk_hbm,
    v_hbm,
    z_hbm,
    cqk_hbm,
    cv_hbm,
    ld_hbm,
    wg_hbm,
    norm_hbm,
    att_hbm,
    roll_hbm,
    len_ref,
    place_ref,
    cqk_ref,
    cv_ref,
    ld_ref,
    wg_ref,
    norm_ref,
    qk,
    v,
    z,
    att,
    rim_qk,
    rim_v,
    xqk,
    xv,
    rows,
    m,
    local,
    carry,
    strict_a,
    strict_b,
    base_a,
    base_b,
    left_a,
    left_b,
    query_a,
    query_b,
    key_a,
    key_b,
    value_a,
    value_b,
    scale_a,
    scale_b,
    aq_0,
    aq_1,
    binp_0,
    binp_1,
    bout_0,
    bout_1,
    step_0,
    step_1,
    maps,
    pair,
    gathered,
    back,
    got,
    enters,
    finals,
    leaving,
    qk_sem,
    v_sem,
    z_sem,
    store_sem,
    rim_send,
    rim_recv,
    pair_send,
    pair_recv,
    x_send,
    x_recv,
    back_send,
    back_recv,
    head_send,
    head_recv,
    own_sem,
    small_sem,
):
    prompts, tok = v.shape[:2]
    heads = ld_ref.shape[1]
    nblk = tok // BLOCK
    half_tok = UNROLL * BLOCK
    chips = gathered.shape[1]
    rows_count = leaving.shape[0]
    seq_count = 2 * chips
    s = lax.axis_index("seq")
    row = lax.axis_index("head")
    core = lax.rem(s, 2)
    chip = lax.div(s, 2)
    mesh_id = pl.DeviceIdType.MESH
    partner = (chip * 2 + 1 - core, row)
    following = (lax.rem(s + 1, seq_count), row)
    preceding = (lax.rem(s + seq_count - 1, seq_count), row)
    sets = {
        1: (strict_b, base_b, left_b, query_b, key_b, value_b, scale_b),
        0: (strict_a, base_a, left_a, query_a, key_a, value_a, scale_a),
    }

    def results(p, half):
        if half == 0:
            return aq_0, binp_0, bout_0, step_0
        return [ref.at[lax.rem(p, 2)] for ref in (aq_1, binp_1, bout_1, step_1)]

    def along_x(d):
        return (lax.rem(chip + d, chips) * 2 + core, row)

    def in_row(d):
        return lax.rem(row + d, rows_count)

    def load_qk(p):
        return pltpu.make_async_copy(qk_hbm.at[p], qk.at[p], qk_sem.at[p])

    def load_v(p):
        return pltpu.make_async_copy(v_hbm.at[p], v.at[p], v_sem.at[p])

    load_z = pltpu.make_async_copy(z_hbm, z, z_sem)
    small = [
        pltpu.make_async_copy(src, dst, small_sem.at[i])
        for i, (src, dst) in enumerate(
            [
                (len_hbm, len_ref),
                (ld_hbm, ld_ref),
                (wg_hbm, wg_ref),
                (cqk_hbm, cqk_ref),
                (cv_hbm, cv_ref),
                (place_hbm, place_ref),
                (norm_hbm, norm_ref),
            ]
        )
    ]
    for copy in small:
        copy.start()
    load_qk(0).start()
    load_v(0).start()
    barrier = pltpu.get_barrier_semaphore()
    peers = [following, preceding]
    peers += [along_x(d) for d in range(1, chips)]
    peers += [(s, in_row(d)) for d in range(1, rows_count)]
    for peer in peers:
        pl.semaphore_signal(barrier, inc=1, device_id=peer, device_id_type=mesh_id)

    before = lax.broadcasted_iota(jnp.int32, (BLOCK, BLOCK), 0)
    after = lax.broadcasted_iota(jnp.int32, (BLOCK, BLOCK), 1)
    lower = before >= after
    strictly = before > after
    upto = jnp.where(before <= after, 1.0, 0.0).astype(F32)
    rows[...] = jnp.zeros_like(rows)
    for copy in small:
        copy.wait()
    position = lax.broadcasted_iota(jnp.int32, (heads, tok), 1) + s * tok
    for p in range(prompts):
        valid = position < len_ref[p]
        log_gate = jnp.where(valid, ld_ref[p], 0.0)
        gain = jnp.where(valid, wg_ref[p], 0.0)
        for c in range(nblk):
            at = 8 * (p * nblk + c)
            rows[at : at + heads, :] = log_gate[:, c * BLOCK : (c + 1) * BLOCK]
            rows[at + heads : at + 2 * heads, :] = gain[:, c * BLOCK : (c + 1) * BLOCK]
    raw_rows = rows[...]
    sums = jnp.dot(raw_rows, upto, precision=lax.Precision.HIGHEST, preferred_element_type=F32)
    kind = lax.broadcasted_iota(jnp.int32, raw_rows.shape, 0) % 8
    rows[...] = jnp.where(kind < heads, sums * LOG2E, raw_rows)
    half_taps_qk = 0.5 * cqk_ref[...].astype(F32)
    half_taps_v = 0.5 * cv_ref[...].astype(F32)
    masks = lane_masks(BASE)
    ones = jnp.ones((DK, DK), BF16)

    def prepare(p, half):
        strict_ref, base_ref, left_ref, query_ref, key_ref, value_ref, scale_ref = sets[half]
        blocks = range(UNROLL)
        start = half * half_tok
        if half == 0:
            scale = jnp.where(s == 0, 0.0, 1.0).astype(F32)
            xqk[0:RIM, :] = rim_qk[p].astype(F32) * scale
        else:
            xqk[0:RIM, :] = qk[p, 2 * start - RIM : 2 * start, :].astype(F32)
        xqk[RIM:, :] = qk[p, 2 * start : 2 * (start + half_tok), :].astype(F32)
        for h in range(heads):
            lanes = slice(h * DV, (h + 1) * DV)
            if half == 0:
                xv[h, 0:RIM, :] = rim_v[p, :, lanes].astype(F32) * scale
            else:
                xv[h, 0:RIM, :] = v[p, start - RIM : start, lanes].astype(F32)
            xv[h, RIM:, :] = v[p, start : start + half_tok, lanes].astype(F32)
        yield

        def mixed(u, which):
            total = None
            for i in range(CONV):
                at = RIM + 2 * (u * BLOCK - (CONV - 1) + i) + which
                term = xqk[pl.ds(at, BLOCK, stride=2), :] * half_taps_qk[i, which : which + 1, :]
                total = term if total is None else total + term
            return silu_of_twice(total)

        squares, mixes = [], []
        for u in blocks:
            mixes.append((mixed(u, 0), mixed(u, 1)))
            both = jnp.concatenate(mixes[u], axis=0)
            squares.append((both * both).astype(BF16))
            yield
        totals = [dot(sq, ones) for sq in squares]
        yield
        keys_t = []
        for u in blocks:
            q, k = mixes[u]
            query_ref[u] = (q * lax.rsqrt(totals[u][:BLOCK] + EPSILON)).astype(BF16)
            k = k * lax.rsqrt(totals[u][BLOCK:] + EPSILON)
            key_ref[u] = k.astype(BF16)
            keys_t.append(k.T.astype(BF16))
            yield
        grams = []
        for u in blocks:
            grams.append(dot(jnp.concatenate([query_ref[u], key_ref[u]], axis=0), keys_t[u]))
            yield
        stricts = []
        for u in blocks:
            at = pl.multiple_of(8 * (p * nblk + half * UNROLL + u), 8)
            tile = rows[pl.ds(at, 8), :]
            column = tile.T
            query_key = jnp.where(lower, grams[u][:BLOCK], 0.0).astype(BF16)
            key_key = jnp.where(strictly, grams[u][BLOCK:], 0.0).astype(BF16)
            for h in range(heads):
                n = u * heads + h
                middle = 0.5 * tile[h : h + 1, BLOCK - 1 : BLOCK]
                gain = tile[heads + h : heads + h + 1].astype(BF16)
                strict = key_key * gain
                stricts.append(strict)
                strict_ref[n] = strict
                left_ref[n, 0:DK, :] = keys_t[u] * gain
                left_ref[n, DK:, :] = query_key * gain
                growth = jnp.exp2(middle - column[:, h : h + 1])
                total = None
                for i in range(CONV):
                    at = RIM + u * BLOCK - (CONV - 1) + i
                    term = xv[h, at : at + BLOCK, :] * half_taps_v[i : i + 1, h * DV : (h + 1) * DV]
                    total = term if total is None else total + term
                value_ref[n] = (silu_of_twice(total) * growth).astype(BF16)
                scale_ref[n : n + 1, :] = jnp.broadcast_to(jnp.exp2(middle), (1, BLOCK))
                yield
        found = yield from base_inverses(stricts, masks)
        for n, x in enumerate(found):
            base_ref[n] = x.astype(BF16)

    def solve(p, half):
        strict_ref, base_ref, left_ref, query_ref, key_ref, value_ref, scale_ref = sets[half]
        aq, binp, bout, step = results(p, half)
        units = range(UNROLL * heads)
        mid = BLOCK // 2
        lows = [strict_ref[n] for n in units]
        inverses = yield from merge_blocks([base_ref[n] for n in units], lows)
        tops = [x[:, :mid] for x in inverses]
        bots = [x[:, mid:] for x in inverses]
        def written(n, block):
            return jnp.concatenate([key_ref[n // heads, block, :], value_ref[n, block, :]], axis=1)

        w1, rest, w2 = [], [], []
        for n in units:
            w1.append(dot(tops[n], written(n, slice(0, mid))).astype(BF16))
            if n % 2:
                yield
        for n in units:
            below = written(n, slice(mid, BLOCK)).astype(F32)
            rest.append((below - dot(lows[n][mid:, :mid], w1[n])).astype(BF16))
            if n % 2:
                yield
        for n in units:
            w2.append(dot(bots[n], rest[n]).astype(BF16))
            if n % 2:
                yield
        for n in units:
            r = dot(left_ref[n], jnp.concatenate([w1[n], w2[n]], axis=0))
            aq[n, 0:DK, :] = (-r[:DK, :DK]).astype(BF16)
            binp[n] = r[:DK, DK:] * scale_ref[n : n + 1, :]
            aq[n, DK:, :] = (query_ref[n // heads].astype(F32) - r[DK:, :DK]).astype(BF16)
            bout[n] = r[DK:, DK:]
            yield
        step[...] = scale_ref[...]

    def advance(p, half):
        aq, binp, bout, step = results(p, half)
        states = [carry[h] for h in range(heads)]
        for u in range(UNROLL):
            tokens = slice(half * half_tok + u * BLOCK, half * half_tok + (u + 1) * BLOCK)
            for h in range(heads):
                n = u * heads + h
                scale = step[n : n + 1, :]
                gate = scale * scale
                chain = p * heads + h
                if half == 0 and u == 0:
                    trans = jnp.where(before == after, 1.0, 0.0) + aq[n, 0:DK, :].astype(F32)
                    states[h] = jnp.concatenate([trans * gate, binp[n]], axis=1)
                    m[chain, tokens, :] = (aq[n, DK:, :].astype(F32) * scale).astype(BF16)
                    local[chain, tokens, :] = bout[n].astype(BF16)
                    continue
                r = dot(aq[n], states[h].astype(BF16))
                wide = jnp.concatenate([gate, gate], axis=1)
                inputs = jnp.concatenate([jnp.zeros((DK, DK), F32), binp[n]], axis=1)
                states[h] = wide * (states[h] + r[:DK]) + inputs
                m[chain, tokens, :] = (r[DK:, :DK] * scale).astype(BF16)
                local[chain, tokens, :] = (r[DK:, DK:] * scale + bout[n]).astype(BF16)
            yield
        for h in range(heads):
            if half == 0:
                carry[h] = states[h]
            else:
                maps[h, p] = states[h].astype(BF16)

    def chain_steps(p):
        yield from advance(p, 0)
        yield from advance(p, 1)

    def swap(p):
        return pltpu.make_async_remote_copy(
            maps.at[1 - core, p],
            pair.at[p],
            pair_send.at[p],
            pair_recv.at[p],
            device_id=partner,
            device_id_type=mesh_id,
        )

    def spread(p, d):
        return pltpu.make_async_remote_copy(
            gathered.at[p, chip],
            gathered.at[p, chip],
            x_send.at[p, d - 1],
            x_recv.at[p, d - 1],
            device_id=along_x(d),
            device_id_type=mesh_id,
        )

    def give_back(p):
        return pltpu.make_async_remote_copy(
            back.at[p],
            got.at[p],
            back_send.at[p],
            back_recv.at[p],
            device_id=partner,
            device_id_type=mesh_id,
        )

    def join_pair(p):
        swap(p).wait_recv()
        own = maps[core, p]
        other = pair[p]
        early = jnp.where(core == 0, own, other)
        late = jnp.where(core == 0, other, own)
        both = dot(late[:, :DK], early)
        joined = jnp.concatenate([both[:, :DK], both[:, DK:] + late[:, DK:].astype(F32)], axis=1)
        gathered[p, chip] = joined.astype(BF16)
        for d in range(1, chips):
            spread(p, d).start()

    def compose(p):
        for d in range(1, chips):
            spread(p, d).wait_recv()
        state = gathered[p, 0][:, DK:].astype(F32)
        enter = jnp.where(chip == 1, state, 0.0)
        for k in range(1, chips):
            tk = gathered[p, k]
            state = dot(tk[:, :DK], state.astype(BF16)) + tk[:, DK:].astype(F32)
            if k < chips - 1:
                enter = jnp.where(chip == k + 1, state, enter)
        first_map = jnp.where(core == 0, maps[core, p], pair[p])
        enter = enter.astype(BF16)
        second = (dot(first_map[:, :DK], enter) + first_map[:, DK:].astype(F32)).astype(BF16)
        final = state.astype(BF16)
        finals[core, p] = final
        enters[core, p] = jnp.where(core == 0, enter, second)
        back[p, 0] = jnp.where(core == 0, second, enter)
        back[p, 1] = final
        give_back(p).start()

    def receive(p):
        give_back(p).wait_recv()
        enters[1 - core, p] = got[p, 0]
        finals[1 - core, p] = got[p, 1]

    norm_gain = norm_ref[...]
    average = jnp.full((DV, DV), 1.0 / DV, BF16)

    def finish(p):
        def part(i, _):
            places, fades, raws = [], [], []
            for u in range(UNROLL):
                c = i * UNROLL + u
                at = pl.ds(pl.multiple_of(c * BLOCK, BLOCK), BLOCK)
                tile = rows[pl.ds(pl.multiple_of(8 * (p * nblk + c), 8), 8), :]
                column = tile.T
                for h in range(heads):
                    n = p * heads + h
                    middle = 0.5 * tile[h : h + 1, BLOCK - 1 : BLOCK]
                    places.append((at, h))
                    fades.append(jnp.exp2(column[:, h : h + 1] - middle))
                    raws.append(dot(m[n, at, :], enters[h, p]) + local[n, at, :].astype(F32))
            raws = [raw * fade for raw, fade in zip(raws, fades)]
            means = [dot((raw * raw).astype(BF16), average) for raw in raws]
            for (at, h), raw, mean in zip(places, raws, means):
                zh = z[p, at, h * DV : (h + 1) * DV].astype(F32)
                gated = raw * lax.rsqrt(mean + EPSILON) * norm_gain * silu(zh)
                att[p, at, h * DV : (h + 1) * DV] = gated.astype(BF16)
            return 0

        lax.fori_loop(0, nblk // UNROLL, part, 0)

    load_qk(0).wait()
    load_v(0).wait()
    for p in range(1, prompts):
        load_qk(p).start()
        load_v(p).start()
    load_z.start()
    interleave((prepare(0, 1), 1))
    pl.semaphore_wait(barrier, len(peers))
    rims = [
        pltpu.make_async_remote_copy(
            src.at[:, pl.ds(src.shape[1] - RIM, RIM), :],
            dst,
            rim_send.at[i],
            rim_recv.at[i],
            device_id=following,
            device_id_type=mesh_id,
        )
        for i, (src, dst) in enumerate([(qk_hbm, rim_qk), (v_hbm, rim_v)])
    ]
    for rim in rims:
        rim.start()
    interleave((solve(0, 1), 1))
    for rim in rims:
        rim.wait()
    interleave((prepare(0, 0), 1))

    def prompt(p, _):
        load_qk(p + 1).wait()
        load_v(p + 1).wait()
        interleave((solve(p, 0), 37), (prepare(p + 1, 1), 38))

        @pl.when(p >= 1)
        def _():
            join_pair(p - 1)

        interleave((solve(p + 1, 1), 37), (prepare(p + 1, 0), 38), (chain_steps(p), 8))
        swap(p).start()
        return 0

    last = prompts - 1
    lax.fori_loop(0, last, prompt, 0)
    interleave((solve(last, 0), 1))
    join_pair(last - 1)
    interleave((chain_steps(last), 1))
    swap(last).start()
    for p in range(last - 1):
        compose(p)
    join_pair(last)
    load_z.wait()
    for p in range(last - 1):
        receive(p)
        finish(p)
    compose(last - 1)
    compose(last)
    receive(last - 1)
    receive(last)
    sends = []
    for d in range(1, rows_count):
        to = in_row(d)
        chosen = place_ref[0, to]
        for h in range(heads):
            leaving[d, h] = finals[h, chosen]
        send = pltpu.make_async_remote_copy(
            leaving.at[d],
            roll_hbm.at[row],
            head_send.at[d],
            head_recv.at[d],
            device_id=(s, to),
            device_id_type=mesh_id,
        )
        send.start()
        sends.append(send)
    chosen = place_ref[0, row]
    for h in range(heads):
        leaving[0, h] = finals[h, chosen]
    keep = pltpu.make_async_copy(leaving.at[0], roll_hbm.at[row], own_sem)
    keep.start()
    finish(last - 1)
    finish(last)
    store = pltpu.make_async_copy(att, att_hbm, store_sem)
    store.start()
    for p in range(prompts):
        swap(p).wait_send()
        for d in range(1, chips):
            spread(p, d).wait_send()
        give_back(p).wait_send()
    for send in sends:
        send.wait()
    keep.wait()
    store.wait()


def delta(lengths, placement, qk, v, z, conv_qk, conv_v, log_decay, write_gain, norm_gain, chips, rows_count):
    prompts, tok, width = v.shape
    heads = width // DV
    chains = prompts * heads
    units = UNROLL * heads
    nblk = tok // BLOCK
    hbm = pl.BlockSpec(memory_space=pl.ANY)
    dma = pltpu.SemaphoreType.DMA

    def twice(*spec):
        return [pltpu.VMEM(*spec), pltpu.VMEM(*spec)]

    return pl.pallas_call(
        delta_kernel,
        in_specs=[hbm] * 10,
        out_specs=[hbm, hbm],
        out_shape=[
            jax.ShapeDtypeStruct((prompts, tok, width), BF16),
            jax.ShapeDtypeStruct((rows_count, heads, DK, DV), BF16),
        ],
        scratch_shapes=[
            pltpu.SMEM(lengths.shape, jnp.int32),
            pltpu.SMEM(placement.shape, jnp.int32),
            pltpu.VMEM(conv_qk.shape, BF16),
            pltpu.VMEM(conv_v.shape, BF16),
            pltpu.VMEM(log_decay.shape, F32),
            pltpu.VMEM(write_gain.shape, F32),
            pltpu.VMEM(norm_gain.shape, F32),
            pltpu.VMEM(qk.shape, BF16),
            pltpu.VMEM(v.shape, BF16),
            pltpu.VMEM(z.shape, BF16),
            pltpu.VMEM(z.shape, BF16),
            pltpu.VMEM((prompts, RIM, DK), BF16),
            pltpu.VMEM((prompts, RIM, width), BF16),
            pltpu.VMEM((RIM + 2 * UNROLL * BLOCK, DK), F32),
            pltpu.VMEM((heads, RIM + UNROLL * BLOCK, DV), F32),
            pltpu.VMEM((8 * prompts * nblk, BLOCK), F32),
            pltpu.VMEM((chains, tok, DK), BF16),
            pltpu.VMEM((chains, tok, DV), BF16),
            pltpu.VMEM((heads, DK, DK + DV), F32),
            *twice((units, BLOCK, BLOCK), BF16),
            *twice((units, BASE, BLOCK), BF16),
            *twice((units, 2 * BLOCK, BLOCK), BF16),
            *twice((UNROLL, BLOCK, DK), BF16),
            *twice((UNROLL, BLOCK, DK), BF16),
            *twice((units, BLOCK, DV), BF16),
            *twice((units, BLOCK), F32),
            pltpu.VMEM((units, 2 * BLOCK, DK), BF16),
            pltpu.VMEM((2, units, 2 * BLOCK, DK), BF16),
            pltpu.VMEM((units, DK, DV), F32),
            pltpu.VMEM((2, units, DK, DV), F32),
            pltpu.VMEM((units, BLOCK, DV), F32),
            pltpu.VMEM((2, units, BLOCK, DV), F32),
            pltpu.VMEM((units, BLOCK), F32),
            pltpu.VMEM((2, units, BLOCK), F32),
            pltpu.VMEM((heads, prompts, DK, DK + DV), BF16),
            pltpu.VMEM((prompts, DK, DK + DV), BF16),
            pltpu.VMEM((prompts, chips, DK, DK + DV), BF16),
            pltpu.VMEM((prompts, 2, DK, DV), BF16),
            pltpu.VMEM((prompts, 2, DK, DV), BF16),
            pltpu.VMEM((heads, prompts, DK, DV), BF16),
            pltpu.VMEM((heads, prompts, DK, DV), BF16),
            pltpu.VMEM((rows_count, heads, DK, DV), BF16),
            dma((prompts,)),
            dma((prompts,)),
            dma,
            dma,
            dma((2,)),
            dma((2,)),
            dma((prompts,)),
            dma((prompts,)),
            dma((prompts, chips - 1)),
            dma((prompts, chips - 1)),
            dma((prompts,)),
            dma((prompts,)),
            dma((rows_count,)),
            dma((rows_count,)),
            dma,
            dma((7,)),
        ],
        compiler_params=pltpu.CompilerParams(
            vmem_limit_bytes=VMEM_LIMIT, collective_id=0, has_side_effects=True
        ),
        name="delta",
    )(lengths, placement, qk, v, z, conv_qk, conv_v, log_decay, write_gain, norm_gain)


def shards(
    qk_in,
    v_in,
    gate_z,
    conv_qk,
    conv_v,
    log_decay,
    write_gain,
    norm_gain,
    prompt_lengths,
    placement,
):
    prompts, tok = v_in.shape[:2]
    heads = log_decay.shape[1]
    head_count = lax.axis_size("head")
    seq_count = lax.axis_size("seq")
    arguments = (
        prompt_lengths,
        placement,
        qk_in.reshape(prompts, 2 * tok, DK),
        v_in,
        gate_z,
        conv_qk,
        conv_v,
        log_decay,
        write_gain,
        norm_gain.reshape(1, DV),
    )
    arguments = [pltpu.with_memory_space_constraint(a, pltpu.HBM) for a in arguments]
    attended, arrived = delta(*arguments, seq_count // 2, head_count)
    position = lax.broadcasted_iota(jnp.int32, attended.shape, 1) + lax.axis_index("seq") * tok
    limit = lax.broadcast_in_dim(prompt_lengths, attended.shape, (0,))
    attended = jnp.where(position < limit, attended, 0).astype(BF16)
    rollout = arrived.astype(F32).reshape(1, 1, head_count * heads, DK, DV)
    return attended, rollout


def solution(mesh):
    return jax.shard_map(
        shards,
        mesh=mesh,
        in_specs=(
            P(None, "seq", None, "head"),
            P(None, "seq", "head"),
            P(None, "seq", "head"),
            P(None, None, "head"),
            P(None, "head"),
            P(None, "head", "seq"),
            P(None, "head", "seq"),
            P(),
            P(),
            P("seq", None),
        ),
        out_specs=(P(None, "seq", "head"), P("seq", "head", None, None, None)),
        check_vma=False,
    )
```

```python
import math

import jax
import jax.numpy as jnp
from jax import lax
from jax.experimental import pallas as pl
from jax.experimental.pallas import tpu as pltpu
from jax.sharding import PartitionSpec as P

DK = 128
DV = 128
CONV = 4
BLOCK = 128
BASE = 16
UNROLL = 4
RIM = 16
EPSILON = 1e-06
LOG2E = 1.4426950408889634
F32 = jnp.float32
BF16 = jnp.bfloat16
VMEM_LIMIT = 40 * 1024 * 1024


def dot(a, b):
    return jnp.dot(a, b, preferred_element_type=F32)


def silu_of_twice(half):
    return half + half * jnp.tanh(half)


def silu(x):
    return silu_of_twice(0.5 * x)


def interleave(*parts):
    parts = [[0, count, steps] for steps, count in parts]
    while parts:
        part = min(parts, key=lambda p: p[0] / p[1])
        part[0] += 1
        try:
            next(part[2])
        except StopIteration:
            parts.remove(part)


def base_inverses(stricts, masks):
    half = BASE // 2
    lane = lax.broadcasted_iota(jnp.int32, (half, BLOCK), 1)
    row = lax.broadcasted_iota(jnp.int32, (half, BLOCK), 0)
    home = lane // BASE
    tops, bots, lows_top, lows_bot = [], [], [], []
    for s in stricts:
        compact = s[0:BASE] * masks[0]
        for b in range(1, BLOCK // BASE):
            compact = compact + s[b * BASE : (b + 1) * BASE] * masks[b]
        compact = compact.astype(F32)
        lows_top.append(compact[:half])
        lows_bot.append(compact[half:])
        tops.append(jnp.where(lane % BASE == row, 1.0, 0.0).astype(F32))
        bots.append(jnp.where(lane % BASE == row + half, 1.0, 0.0).astype(F32))
    yield
    for j in range(BASE - 1):
        index = home * BASE + j
        for n in range(len(stricts)):
            source = tops[n][j : j + 1] if j < half else bots[n][j - half : j - half + 1]
            if j < half - 1:
                tops[n] = tops[n] - jnp.take_along_axis(lows_top[n], index, axis=1) * source
            bots[n] = bots[n] - jnp.take_along_axis(lows_bot[n], index, axis=1) * source
        yield
    return [jnp.concatenate([t, b], axis=0) for t, b in zip(tops, bots)]


def lane_masks(size):
    home = lax.broadcasted_iota(jnp.int32, (size, BLOCK), 1) // size
    return [jnp.where(home == b, 1.0, 0.0).astype(BF16) for b in range(BLOCK // size)]


def stacked_products(lefts, rights):
    out = []
    for n in range(0, len(lefts), 2):
        size = lefts[n].shape[0]
        both = dot(
            jnp.concatenate(lefts[n : n + 2], axis=0), jnp.concatenate(rights[n : n + 2], axis=1)
        )
        out += [both[:size, :BLOCK].astype(BF16), both[size:, BLOCK:].astype(BF16)]
        yield
    return out


def merge_blocks(inverses, lows):
    size = BASE
    while size < BLOCK // 2:
        masks = lane_masks(size)
        count = BLOCK // size
        evens = sum(masks[2::2], masks[0])
        odds = sum(masks[3::2], masks[1])
        zeros = jnp.zeros((size, BLOCK), BF16)
        below = [
            jnp.concatenate(
                [
                    low[o * size : (o + 1) * size] * masks[o - 1] if o % 2 else zeros
                    for o in range(count)
                ],
                axis=0,
            )
            for low in lows
        ]
        above = [
            jnp.concatenate([zeros if e % 2 else x * masks[e] for e in range(count)], axis=0)
            for x in inverses
        ]
        ys = yield from stacked_products(inverses, below)
        zs = yield from stacked_products(ys, above)
        inverses = [
            jnp.concatenate([x * evens, x * odds - z], axis=0) for x, z in zip(inverses, zs)
        ]
        size *= 2
    return inverses


def delta_kernel(
    len_hbm,
    place_hbm,
    qk_hbm,
    v_hbm,
    z_hbm,
    cqk_hbm,
    cv_hbm,
    ld_hbm,
    wg_hbm,
    norm_hbm,
    att_hbm,
    roll_hbm,
    len_ref,
    place_ref,
    cqk_ref,
    cv_ref,
    ld_ref,
    wg_ref,
    norm_ref,
    qk,
    v,
    z,
    att,
    rim_qk,
    rim_v,
    xqk,
    xv,
    rows,
    m,
    local,
    carry,
    strict_a,
    strict_b,
    base_a,
    base_b,
    left_a,
    left_b,
    query_a,
    query_b,
    key_a,
    key_b,
    value_a,
    value_b,
    scale_a,
    scale_b,
    aq_0,
    aq_1,
    binp_0,
    binp_1,
    bout_0,
    bout_1,
    step_0,
    step_1,
    maps,
    pair,
    gathered,
    back,
    got,
    enters,
    by_y,
    by_z,
    picked,
    handed,
    wish,
    wished,
    qk_sem,
    v_sem,
    z_sem,
    store_sem,
    rim_send,
    rim_recv,
    pair_send,
    pair_recv,
    x_send,
    x_recv,
    back_send,
    back_recv,
    near_send,
    near_recv,
    far_send,
    far_recv,
    hand_send,
    hand_recv,
    keep_sem,
    wish_send,
    wish_recv,
    small_sem,
):
    prompts, tok = v.shape[:2]
    heads = ld_ref.shape[1]
    nblk = tok // BLOCK
    half_tok = UNROLL * BLOCK
    chips = gathered.shape[1]
    side = by_y.shape[1]
    seq_count = 2 * chips
    s = lax.axis_index("seq")
    row = lax.axis_index("head")
    core = lax.rem(s, 2)
    chip = lax.div(s, 2)
    mesh_id = pl.DeviceIdType.MESH
    partner = (chip * 2 + 1 - core, row)
    following = (lax.rem(s + 1, seq_count), row)
    preceding = (lax.rem(s + seq_count - 1, seq_count), row)
    sets = {
        1: (strict_b, base_b, left_b, query_b, key_b, value_b, scale_b),
        0: (strict_a, base_a, left_a, query_a, key_a, value_a, scale_a),
    }

    def results(p, half):
        if half == 0:
            return aq_0, binp_0, bout_0, step_0
        return [ref.at[lax.rem(p, 2)] for ref in (aq_1, binp_1, bout_1, step_1)]

    def along_x(d):
        return (lax.rem(chip + d, chips) * 2 + core, row)

    at_y = lax.div(row, side)
    at_z = lax.rem(row, side)

    def along_y(d):
        return (s, lax.rem(at_y + d, side) * side + at_z)

    def along_z(d):
        return (s, at_y * side + lax.rem(at_z + d, side))

    def load_qk(p):
        return pltpu.make_async_copy(qk_hbm.at[p], qk.at[p], qk_sem.at[p])

    def load_v(p):
        return pltpu.make_async_copy(v_hbm.at[p], v.at[p], v_sem.at[p])

    load_z = pltpu.make_async_copy(z_hbm, z, z_sem)
    small = [
        pltpu.make_async_copy(src, dst, small_sem.at[i])
        for i, (src, dst) in enumerate(
            [
                (len_hbm, len_ref),
                (ld_hbm, ld_ref),
                (wg_hbm, wg_ref),
                (cqk_hbm, cqk_ref),
                (cv_hbm, cv_ref),
                (place_hbm, place_ref),
                (norm_hbm, norm_ref),
            ]
        )
    ]
    for copy in small:
        copy.start()
    load_qk(0).start()
    load_v(0).start()
    barrier = pltpu.get_barrier_semaphore()
    peers = [following, preceding]
    peers += [along_x(d) for d in range(1, chips)]
    peers += [along_y(d) for d in range(1, side)]
    peers += [along_z(d) for d in range(1, side)]
    for peer in peers:
        pl.semaphore_signal(barrier, inc=1, device_id=peer, device_id_type=mesh_id)

    before = lax.broadcasted_iota(jnp.int32, (BLOCK, BLOCK), 0)
    after = lax.broadcasted_iota(jnp.int32, (BLOCK, BLOCK), 1)
    lower = before >= after
    strictly = before > after
    upto = jnp.where(before <= after, 1.0, 0.0).astype(F32)
    rows[...] = jnp.zeros_like(rows)
    for copy in small:
        copy.wait()
    position = lax.broadcasted_iota(jnp.int32, (heads, tok), 1) + s * tok
    for p in range(prompts):
        valid = position < len_ref[p]
        log_gate = jnp.where(valid, ld_ref[p], 0.0)
        gain = jnp.where(valid, wg_ref[p], 0.0)
        for c in range(nblk):
            at = 8 * (p * nblk + c)
            rows[at : at + heads, :] = log_gate[:, c * BLOCK : (c + 1) * BLOCK]
            rows[at + heads : at + 2 * heads, :] = gain[:, c * BLOCK : (c + 1) * BLOCK]
    raw_rows = rows[...]
    sums = jnp.dot(raw_rows, upto, precision=lax.Precision.HIGHEST, preferred_element_type=F32)
    kind = lax.broadcasted_iota(jnp.int32, raw_rows.shape, 0) % 8
    rows[...] = jnp.where(kind < heads, sums * LOG2E, raw_rows)
    half_taps_qk = 0.5 * cqk_ref[...].astype(F32)
    half_taps_v = 0.5 * cv_ref[...].astype(F32)
    masks = lane_masks(BASE)
    ones = jnp.ones((DK, DK), BF16)

    def prepare(p, half):
        strict_ref, base_ref, left_ref, query_ref, key_ref, value_ref, scale_ref = sets[half]
        blocks = range(UNROLL)
        start = half * half_tok
        if half == 0:
            scale = jnp.where(s == 0, 0.0, 1.0).astype(F32)
            xqk[0:RIM, :] = rim_qk[p].astype(F32) * scale
        else:
            xqk[0:RIM, :] = qk[p, 2 * start - RIM : 2 * start, :].astype(F32)
        xqk[RIM:, :] = qk[p, 2 * start : 2 * (start + half_tok), :].astype(F32)
        for h in range(heads):
            lanes = slice(h * DV, (h + 1) * DV)
            if half == 0:
                xv[h, 0:RIM, :] = rim_v[p, :, lanes].astype(F32) * scale
            else:
                xv[h, 0:RIM, :] = v[p, start - RIM : start, lanes].astype(F32)
            xv[h, RIM:, :] = v[p, start : start + half_tok, lanes].astype(F32)
        yield

        def mixed(u, which):
            total = None
            for i in range(CONV):
                at = RIM + 2 * (u * BLOCK - (CONV - 1) + i) + which
                term = xqk[pl.ds(at, BLOCK, stride=2), :] * half_taps_qk[i, which : which + 1, :]
                total = term if total is None else total + term
            return silu_of_twice(total)

        squares, mixes = [], []
        for u in blocks:
            mixes.append((mixed(u, 0), mixed(u, 1)))
            both = jnp.concatenate(mixes[u], axis=0)
            squares.append((both * both).astype(BF16))
            yield
        totals = [dot(sq, ones) for sq in squares]
        yield
        keys_t = []
        for u in blocks:
            q, k = mixes[u]
            query_ref[u] = (q * lax.rsqrt(totals[u][:BLOCK] + EPSILON)).astype(BF16)
            k = k * lax.rsqrt(totals[u][BLOCK:] + EPSILON)
            key_ref[u] = k.astype(BF16)
            keys_t.append(k.T.astype(BF16))
            yield
        grams = []
        for u in blocks:
            grams.append(dot(jnp.concatenate([query_ref[u], key_ref[u]], axis=0), keys_t[u]))
            yield
        stricts = []
        for u in blocks:
            at = pl.multiple_of(8 * (p * nblk + half * UNROLL + u), 8)
            tile = rows[pl.ds(at, 8), :]
            column = tile.T
            query_key = jnp.where(lower, grams[u][:BLOCK], 0.0).astype(BF16)
            key_key = jnp.where(strictly, grams[u][BLOCK:], 0.0).astype(BF16)
            for h in range(heads):
                n = u * heads + h
                middle = 0.5 * tile[h : h + 1, BLOCK - 1 : BLOCK]
                gain = tile[heads + h : heads + h + 1].astype(BF16)
                strict = key_key * gain
                stricts.append(strict)
                strict_ref[n] = strict
                left_ref[n, 0:DK, :] = keys_t[u] * gain
                left_ref[n, DK:, :] = query_key * gain
                growth = jnp.exp2(middle - column[:, h : h + 1])
                total = None
                for i in range(CONV):
                    at = RIM + u * BLOCK - (CONV - 1) + i
                    term = xv[h, at : at + BLOCK, :] * half_taps_v[i : i + 1, h * DV : (h + 1) * DV]
                    total = term if total is None else total + term
                value_ref[n] = (silu_of_twice(total) * growth).astype(BF16)
                scale_ref[n : n + 1, :] = jnp.broadcast_to(jnp.exp2(middle), (1, BLOCK))
                yield
        found = yield from base_inverses(stricts, masks)
        for n, x in enumerate(found):
            base_ref[n] = x.astype(BF16)

    def solve(p, half):
        strict_ref, base_ref, left_ref, query_ref, key_ref, value_ref, scale_ref = sets[half]
        aq, binp, bout, step = results(p, half)
        units = range(UNROLL * heads)
        mid = BLOCK // 2
        lows = [strict_ref[n] for n in units]
        inverses = yield from merge_blocks([base_ref[n] for n in units], lows)
        tops = [x[:, :mid] for x in inverses]
        bots = [x[:, mid:] for x in inverses]
        def written(n, block):
            return jnp.concatenate([key_ref[n // heads, block, :], value_ref[n, block, :]], axis=1)

        w1, rest, w2 = [], [], []
        for n in units:
            w1.append(dot(tops[n], written(n, slice(0, mid))).astype(BF16))
            if n % 2:
                yield
        for n in units:
            below = written(n, slice(mid, BLOCK)).astype(F32)
            rest.append((below - dot(lows[n][mid:, :mid], w1[n])).astype(BF16))
            if n % 2:
                yield
        for n in units:
            w2.append(dot(bots[n], rest[n]).astype(BF16))
            if n % 2:
                yield
        for n in units:
            r = dot(left_ref[n], jnp.concatenate([w1[n], w2[n]], axis=0))
            aq[n, 0:DK, :] = (-r[:DK, :DK]).astype(BF16)
            binp[n] = r[:DK, DK:] * scale_ref[n : n + 1, :]
            aq[n, DK:, :] = (query_ref[n // heads].astype(F32) - r[DK:, :DK]).astype(BF16)
            bout[n] = r[DK:, DK:]
            yield
        step[...] = scale_ref[...]

    def advance(p, half):
        aq, binp, bout, step = results(p, half)
        states = [carry[h] for h in range(heads)]
        for u in range(UNROLL):
            tokens = slice(half * half_tok + u * BLOCK, half * half_tok + (u + 1) * BLOCK)
            for h in range(heads):
                n = u * heads + h
                scale = step[n : n + 1, :]
                gate = scale * scale
                chain = p * heads + h
                if half == 0 and u == 0:
                    trans = jnp.where(before == after, 1.0, 0.0) + aq[n, 0:DK, :].astype(F32)
                    states[h] = jnp.concatenate([trans * gate, binp[n]], axis=1)
                    m[chain, tokens, :] = (aq[n, DK:, :].astype(F32) * scale).astype(BF16)
                    local[chain, tokens, :] = bout[n].astype(BF16)
                    continue
                r = dot(aq[n], states[h].astype(BF16))
                wide = jnp.concatenate([gate, gate], axis=1)
                inputs = jnp.concatenate([jnp.zeros((DK, DK), F32), binp[n]], axis=1)
                states[h] = wide * (states[h] + r[:DK]) + inputs
                m[chain, tokens, :] = (r[DK:, :DK] * scale).astype(BF16)
                local[chain, tokens, :] = (r[DK:, DK:] * scale + bout[n]).astype(BF16)
            yield
        for h in range(heads):
            if half == 0:
                carry[h] = states[h]
            else:
                maps[h, p] = states[h].astype(BF16)

    def chain_steps(p):
        yield from advance(p, 0)
        yield from advance(p, 1)

    def swap(p):
        return pltpu.make_async_remote_copy(
            maps.at[1 - core, p],
            pair.at[p],
            pair_send.at[p],
            pair_recv.at[p],
            device_id=partner,
            device_id_type=mesh_id,
        )

    def spread(p, d):
        return pltpu.make_async_remote_copy(
            gathered.at[p, chip],
            gathered.at[p, chip],
            x_send.at[p, d - 1],
            x_recv.at[p, d - 1],
            device_id=along_x(d),
            device_id_type=mesh_id,
        )

    def give_back(p):
        return pltpu.make_async_remote_copy(
            back.at[p],
            got.at[p],
            back_send.at[p],
            back_recv.at[p],
            device_id=partner,
            device_id_type=mesh_id,
        )

    def join_pair(p):
        swap(p).wait_recv()
        own = maps[core, p]
        other = pair[p]
        early = jnp.where(core == 0, own, other)
        late = jnp.where(core == 0, other, own)
        both = dot(late[:, :DK], early)
        joined = jnp.concatenate([both[:, :DK], both[:, DK:] + late[:, DK:].astype(F32)], axis=1)
        gathered[p, chip] = joined.astype(BF16)
        for d in range(1, chips):
            spread(p, d).start()

    def compose(p):
        for d in range(1, chips):
            spread(p, d).wait_recv()
        state = gathered[p, 0][:, DK:].astype(F32)
        enter = jnp.where(chip == 1, state, 0.0)
        for k in range(1, chips):
            tk = gathered[p, k]
            state = dot(tk[:, :DK], state.astype(BF16)) + tk[:, DK:].astype(F32)
            if k < chips - 1:
                enter = jnp.where(chip == k + 1, state, enter)
        first_map = jnp.where(core == 0, maps[core, p], pair[p])
        enter = enter.astype(BF16)
        second = (dot(first_map[:, :DK], enter) + first_map[:, DK:].astype(F32)).astype(BF16)
        final = state.astype(BF16)
        mid = DK // 2
        by_y[p, at_y, at_z] = final[:mid]
        by_z[p, at_z, at_y] = final[mid:]
        for copy in near(p):
            copy.start()
        enters[core, p] = jnp.where(core == 0, enter, second)
        back[p] = jnp.where(core == 0, second, enter)
        give_back(p).start()

    def near(p):
        copies = []
        for d in range(1, side):
            for way, (block, to) in enumerate(
                [(by_y.at[p, at_y, at_z], along_z(d)), (by_z.at[p, at_z, at_y], along_y(d))]
            ):
                copies.append(
                    pltpu.make_async_remote_copy(
                        block,
                        block,
                        near_send.at[p, way, d - 1],
                        near_recv.at[p, way, d - 1],
                        device_id=to,
                        device_id_type=mesh_id,
                    )
                )
        return copies

    def far(p):
        copies = []
        for d in range(1, side):
            for way, (block, to) in enumerate(
                [(by_y.at[p, at_y], along_y(d)), (by_z.at[p, at_z], along_z(d))]
            ):
                copies.append(
                    pltpu.make_async_remote_copy(
                        block,
                        block,
                        far_send.at[p, way, d - 1],
                        far_recv.at[p, way, d - 1],
                        device_id=to,
                        device_id_type=mesh_id,
                    )
                )
        return copies

    def relay(p):
        for copy in near(p):
            copy.wait_recv()
        for copy in far(p):
            copy.start()

    def spot(way, i):
        if way == 0:
            return roll_hbm.at[i, :, core, 0 : DK // 2]
        return roll_hbm.at[:, i, core, DK // 2 : DK]

    def line(way, d):
        return lax.rem((at_y, at_z)[way] + d, side)

    def hand(way, d):
        i = line(way, d)
        return pltpu.make_async_remote_copy(
            handed.at[way, i],
            spot(way, i),
            hand_send.at[way, d],
            hand_recv.at[way, d],
            device_id=partner,
            device_id_type=mesh_id,
        )

    def keep(way, d):
        i = line(way, d)
        return pltpu.make_async_copy(picked.at[way, i], spot(way, i), keep_sem.at[way, d])

    def pick(chosen, target, way, d):
        i = line(way, d)
        blocks = (by_y, by_z)[way]
        for at in range(side):
            block = blocks[0, i, at]
            for p in range(1, prompts):
                block = jnp.where(chosen == p, blocks[p, i, at], block)
            target[way, i, at] = block

    def receive(p):
        give_back(p).wait_recv()
        enters[1 - core, p] = got[p]

    norm_gain = norm_ref[...]
    average = jnp.full((DV, DV), 1.0 / DV, BF16)

    def finish(p):
        def part(i, _):
            places, fades, raws = [], [], []
            for u in range(UNROLL):
                c = i * UNROLL + u
                at = pl.ds(pl.multiple_of(c * BLOCK, BLOCK), BLOCK)
                tile = rows[pl.ds(pl.multiple_of(8 * (p * nblk + c), 8), 8), :]
                column = tile.T
                for h in range(heads):
                    n = p * heads + h
                    middle = 0.5 * tile[h : h + 1, BLOCK - 1 : BLOCK]
                    places.append((at, h))
                    fades.append(jnp.exp2(column[:, h : h + 1] - middle))
                    raws.append(dot(m[n, at, :], enters[h, p]) + local[n, at, :].astype(F32))
            raws = [raw * fade for raw, fade in zip(raws, fades)]
            means = [dot((raw * raw).astype(BF16), average) for raw in raws]
            for (at, h), raw, mean in zip(places, raws, means):
                zh = z[p, at, h * DV : (h + 1) * DV].astype(F32)
                gated = raw * lax.rsqrt(mean + EPSILON) * norm_gain * silu(zh)
                att[p, at, h * DV : (h + 1) * DV] = gated.astype(BF16)
            return 0

        lax.fori_loop(0, nblk // UNROLL, part, 0)

    load_qk(0).wait()
    load_v(0).wait()
    for p in range(1, prompts):
        load_qk(p).start()
        load_v(p).start()
    load_z.start()
    interleave((prepare(0, 1), 1))
    pl.semaphore_wait(barrier, len(peers))
    rims = [
        pltpu.make_async_remote_copy(
            src.at[:, pl.ds(src.shape[1] - RIM, RIM), :],
            dst,
            rim_send.at[i],
            rim_recv.at[i],
            device_id=following,
            device_id_type=mesh_id,
        )
        for i, (src, dst) in enumerate([(qk_hbm, rim_qk), (v_hbm, rim_v)])
    ]
    for rim in rims:
        rim.start()
    interleave((solve(0, 1), 1))
    for rim in rims:
        rim.wait()
    interleave((prepare(0, 0), 1))

    tell = pltpu.make_async_remote_copy(
        wish, wished, wish_send, wish_recv, device_id=partner, device_id_type=mesh_id
    )
    wish[...] = jnp.full(wish.shape, place_ref[0, row], jnp.int32)
    tell.start()

    def prompt(p, _):
        load_qk(p + 1).wait()
        load_v(p + 1).wait()
        interleave((solve(p, 0), 37), (prepare(p + 1, 1), 38))

        @pl.when(p >= 1)
        def _():
            join_pair(p - 1)

        @pl.when(p >= 2)
        def _():
            compose(p - 2)

        interleave((solve(p + 1, 1), 37), (prepare(p + 1, 0), 38), (chain_steps(p), 8))
        swap(p).start()

        @pl.when(p >= 2)
        def _():
            relay(p - 2)

        return 0

    last = prompts - 1
    lax.fori_loop(0, last, prompt, 0)
    interleave((solve(last, 0), 1))
    join_pair(last - 1)
    compose(last - 2)
    interleave((chain_steps(last), 1))
    swap(last).start()
    load_z.wait()
    relay(last - 2)
    receive(0)
    finish(0)
    join_pair(last)
    compose(last - 1)
    receive(1)
    finish(1)
    relay(last - 1)
    compose(last)
    receive(last - 1)
    finish(last - 1)
    relay(last)
    tell.wait()
    theirs = wished[0, 0]
    mine = place_ref[0, row]
    for p in range(last):
        for copy in far(p):
            copy.wait_recv()
    for way in range(2):
        pick(theirs, handed, way, 0)
        hand(way, 0).start()
    receive(last)
    finish(last)
    store = pltpu.make_async_copy(att, att_hbm, store_sem)
    store.start()
    arriving = far(last)
    for d in range(1, side):
        for way in range(2):
            arriving[2 * (d - 1) + way].wait_recv()
            pick(theirs, handed, way, side - d)
            hand(way, side - d).start()
    for d in range(side):
        for way in range(2):
            pick(mine, picked, way, d)
            keep(way, d).start()
    for p in range(prompts):
        swap(p).wait_send()
        for d in range(1, chips):
            spread(p, d).wait_send()
        give_back(p).wait_send()
        for copy in near(p) + far(p):
            copy.wait_send()
    for d in range(side):
        for way in range(2):
            keep(way, d).wait()
            hand(way, d).wait()
    store.wait()


def delta(lengths, placement, qk, v, z, conv_qk, conv_v, log_decay, write_gain, norm_gain, chips, rows_count):
    prompts, tok, width = v.shape
    heads = width // DV
    chains = prompts * heads
    units = UNROLL * heads
    nblk = tok // BLOCK
    side = math.isqrt(rows_count)
    hbm = pl.BlockSpec(memory_space=pl.ANY)
    dma = pltpu.SemaphoreType.DMA

    def twice(*spec):
        return [pltpu.VMEM(*spec), pltpu.VMEM(*spec)]

    return pl.pallas_call(
        delta_kernel,
        in_specs=[hbm] * 10,
        out_specs=[hbm, hbm],
        out_shape=[
            jax.ShapeDtypeStruct((prompts, tok, width), BF16),
            jax.ShapeDtypeStruct((side, side, heads, DK, DV), BF16),
        ],
        scratch_shapes=[
            pltpu.SMEM(lengths.shape, jnp.int32),
            pltpu.SMEM(placement.shape, jnp.int32),
            pltpu.VMEM(conv_qk.shape, BF16),
            pltpu.VMEM(conv_v.shape, BF16),
            pltpu.VMEM(log_decay.shape, F32),
            pltpu.VMEM(write_gain.shape, F32),
            pltpu.VMEM(norm_gain.shape, F32),
            pltpu.VMEM(qk.shape, BF16),
            pltpu.VMEM(v.shape, BF16),
            pltpu.VMEM(z.shape, BF16),
            pltpu.VMEM(z.shape, BF16),
            pltpu.VMEM((prompts, RIM, DK), BF16),
            pltpu.VMEM((prompts, RIM, width), BF16),
            pltpu.VMEM((RIM + 2 * UNROLL * BLOCK, DK), F32),
            pltpu.VMEM((heads, RIM + UNROLL * BLOCK, DV), F32),
            pltpu.VMEM((8 * prompts * nblk, BLOCK), F32),
            pltpu.VMEM((chains, tok, DK), BF16),
            pltpu.VMEM((chains, tok, DV), BF16),
            pltpu.VMEM((heads, DK, DK + DV), F32),
            *twice((units, BLOCK, BLOCK), BF16),
            *twice((units, BASE, BLOCK), BF16),
            *twice((units, 2 * BLOCK, BLOCK), BF16),
            *twice((UNROLL, BLOCK, DK), BF16),
            *twice((UNROLL, BLOCK, DK), BF16),
            *twice((units, BLOCK, DV), BF16),
            *twice((units, BLOCK), F32),
            pltpu.VMEM((units, 2 * BLOCK, DK), BF16),
            pltpu.VMEM((2, units, 2 * BLOCK, DK), BF16),
            pltpu.VMEM((units, DK, DV), F32),
            pltpu.VMEM((2, units, DK, DV), F32),
            pltpu.VMEM((units, BLOCK, DV), F32),
            pltpu.VMEM((2, units, BLOCK, DV), F32),
            pltpu.VMEM((units, BLOCK), F32),
            pltpu.VMEM((2, units, BLOCK), F32),
            pltpu.VMEM((heads, prompts, DK, DK + DV), BF16),
            pltpu.VMEM((prompts, DK, DK + DV), BF16),
            pltpu.VMEM((prompts, chips, DK, DK + DV), BF16),
            pltpu.VMEM((prompts, DK, DV), BF16),
            pltpu.VMEM((prompts, DK, DV), BF16),
            pltpu.VMEM((heads, prompts, DK, DV), BF16),
            pltpu.VMEM((prompts, side, side, DK // 2, DV), BF16),
            pltpu.VMEM((prompts, side, side, DK // 2, DV), BF16),
            pltpu.VMEM((2, side, side, DK // 2, DV), BF16),
            pltpu.VMEM((2, side, side, DK // 2, DV), BF16),
            pltpu.VMEM((8, 128), jnp.int32),
            pltpu.VMEM((8, 128), jnp.int32),
            dma((prompts,)),
            dma((prompts,)),
            dma,
            dma,
            dma((2,)),
            dma((2,)),
            dma((prompts,)),
            dma((prompts,)),
            dma((prompts, chips - 1)),
            dma((prompts, chips - 1)),
            dma((prompts,)),
            dma((prompts,)),
            dma((prompts, 2, side - 1)),
            dma((prompts, 2, side - 1)),
            dma((prompts, 2, side - 1)),
            dma((prompts, 2, side - 1)),
            dma((2, side)),
            dma((2, side)),
            dma((2, side)),
            dma,
            dma,
            dma((7,)),
        ],
        compiler_params=pltpu.CompilerParams(
            vmem_limit_bytes=VMEM_LIMIT, collective_id=0, has_side_effects=True
        ),
        name="delta",
    )(lengths, placement, qk, v, z, conv_qk, conv_v, log_decay, write_gain, norm_gain)


def shards(
    qk_in,
    v_in,
    gate_z,
    conv_qk,
    conv_v,
    log_decay,
    write_gain,
    norm_gain,
    prompt_lengths,
    placement,
):
    prompts, tok = v_in.shape[:2]
    heads = log_decay.shape[1]
    head_count = lax.axis_size("head")
    seq_count = lax.axis_size("seq")
    arguments = (
        prompt_lengths,
        placement,
        qk_in.reshape(prompts, 2 * tok, DK),
        v_in,
        gate_z,
        conv_qk,
        conv_v,
        log_decay,
        write_gain,
        norm_gain.reshape(1, DV),
    )
    arguments = [pltpu.with_memory_space_constraint(a, pltpu.HBM) for a in arguments]
    attended, arrived = delta(*arguments, seq_count // 2, head_count)
    position = lax.broadcasted_iota(jnp.int32, attended.shape, 1) + lax.axis_index("seq") * tok
    limit = lax.broadcast_in_dim(prompt_lengths, attended.shape, (0,))
    attended = jnp.where(position < limit, attended, 0).astype(BF16)
    rollout = arrived.astype(F32).reshape(1, 1, head_count * heads, DK, DV)
    return attended, rollout


def solution(mesh):
    return jax.shard_map(
        shards,
        mesh=mesh,
        in_specs=(
            P(None, "seq", None, "head"),
            P(None, "seq", "head"),
            P(None, "seq", "head"),
            P(None, None, "head"),
            P(None, "head"),
            P(None, "head", "seq"),
            P(None, "head", "seq"),
            P(),
            P(),
            P("seq", None),
        ),
        out_specs=(P(None, "seq", "head"), P("seq", "head", None, None, None)),
        check_vma=False,
    )
```
